256 devices in a mesh: fsdp: 16 (over y_lo, z), sample: 16 (over y_hi, x, core).
Axes of the slice: x: 4, y: 4 (y_hi: 2, y_lo: 2; y = y_hi * 2 + y_lo), z: 8, core: 2. Of those that a mesh axis runs over, the one named last changes fastest.
Arguments:
- hidden: bfloat16 [4, 256, 16, 5120], P(None, 'fsdp', 'sample'), may hold values from -6 to 6
- norm_gain: float32 [5120], replicated, may hold values from 0.5 to 1.5
- w_qkv: bfloat16 [5120, 5120], P(None, 'fsdp'), may hold values from -0.078125 to 0.078125
- query_gain: float32 [128], replicated, may hold values from 0.5 to 5
- key_gain: float32 [128], replicated, may hold values from 0.5 to 4
- prompt_kv: bfloat16 [16, 128, 64, 1024], P('fsdp', 'sample')
- block_table: int32 [16, 16, 8], P('fsdp', 'sample'), may hold values from 0 to 7, as said below
- prompt_slot: int32 [16, 16], P('fsdp'), may hold values from 0 to 15, each once within a row
- prompt_len: int32 [16, 16], P('fsdp'), may hold values from 1 to 512
- resp_kv: bfloat16 [256, 16, 128, 1024], P('fsdp', 'sample')
- resp_len: int32 [256, 16], P('fsdp', 'sample'), may hold values from 1 to 128
Outputs:
- attention: bfloat16 [4, 256, 16, 4096], P(None, 'fsdp', 'sample')
The draws below stay inside these ranges and needn't reach their ends.
Inputs may be any that keep to these rules, and one draw needn't show every extreme that they name: `block_table`: the rows of slots j * 1 to (j + 1) - 1 of a group, together, name each of the 8 pages of pool rows j * 8 onward exactly once.
All inputs are finite; a program needn't handle non-finite values.
Results may differ from the reference program's by a relative error of at most 0.019.
The reference program's roundings to bfloat16 on the way (of `normed`, `projected`, `queries`, `key_new` and `prefix_kv`) count: a program that leaves them out, or rounds other values in their place, can miss the bound.
Values may be sent and summed in bfloat16 or wider, within the bound.
No kernel may reach another device: no remote copies, remote signals or barrier semaphores. Data moves between devices by JAX's collectives and lax.ppermute only.
A program may use at most 128 MiB of HBM per device.

```python
import math
import jax
import jax.numpy as jnp
from jax import lax

D = 5120
HD = 128
HEADS = 32
KV_HEADS = 4
STEPS = 4
BLOCK = 64
PAGES = 8
RL = 128
OWN_DEV = 1
PROMPTS_DEV = 16
PROMPTS = 256
SAMPLES = 16
GROUPS = 16
POOL = 128
PLEN = 512
QD = 4096
KVD = 512


def scaled_rows(key, shape, low_scale, high_scale):
    first_key, second_key = jax.random.split(key)
    base = jax.random.normal(first_key, shape, jnp.float32)
    logs = jax.random.uniform(second_key, shape[:-1] + (1,), jnp.float32, jnp.log(low_scale), jnp.log(high_scale))
    return base * jnp.exp(logs)


def draw_query_gain(key, part):
    key = jax.random.fold_in(key, 12)
    values_out = jax.random.uniform(key, (HD,), jnp.float32, 0.5, 2.0)
    return values_out


def draw_prompt_kv(key, part):
    key = jax.random.fold_in(key, 11)
    values_out = scaled_rows(key, (GROUPS, POOL, BLOCK, 2 * KVD), 0.5, 2.0)
    return values_out.astype(jnp.bfloat16)


def draw_resp_kv(key, part):
    key = jax.random.fold_in(key, 16)
    values_out = scaled_rows(key, (PROMPTS, SAMPLES, RL, 2 * KVD), 0.5, 2.0)
    return values_out.astype(jnp.bfloat16)


def draw_block_table(key, part):
    key = jax.random.fold_in(key, 13)
    holders = PROMPTS_DEV // OWN_DEV
    subkeys = jax.random.split(key, GROUPS * holders)
    orders = jax.vmap(lambda subkey: jax.random.permutation(subkey, OWN_DEV * PAGES))(subkeys)
    return orders.reshape(GROUPS, PROMPTS_DEV, PAGES).astype(jnp.int32)


def draw_prompt_len(key, part):
    key = jax.random.fold_in(key, 14)
    first_key, second_key = jax.random.split(key)
    lengths = jax.random.randint(first_key, (GROUPS, PROMPTS_DEV), 1, PLEN + 1, jnp.int32)
    chosen = jax.random.randint(second_key, (GROUPS,), 0, PROMPTS_DEV, jnp.int32)
    lengths = lengths.at[jnp.arange(GROUPS), chosen].set(PLEN)
    return lengths.astype(jnp.int32)


def draw_resp_len(key, part):
    key = jax.random.fold_in(key, 15)
    first_key, second_key, third_key = jax.random.split(key, 3)
    one_draw = jax.random.randint(first_key, (PROMPTS, SAMPLES), 1, RL + 1, jnp.int32)
    two_draw = jax.random.randint(second_key, (PROMPTS, SAMPLES), 1, RL + 1, jnp.int32)
    lengths = jnp.minimum(one_draw, two_draw)
    chosen = jax.random.randint(third_key, (GROUPS, 2), 0, PROMPTS_DEV, jnp.int32)
    row_ids = jnp.arange(GROUPS, dtype=jnp.int32) * PROMPTS_DEV + chosen[:, 0]
    column_ids = chosen[:, 1] % SAMPLES
    lengths = lengths.at[row_ids, column_ids].set(RL)
    return lengths.astype(jnp.int32)


def block_scale(stream_key, dims, shards, smallest, top_value):
    def one(dim, parts):
        heights = jax.random.uniform(jax.random.fold_in(jax.random.fold_in(stream_key, 6), dim), (parts,), jnp.float32, smallest / len(shards), top_value / len(shards))
        return jnp.repeat(jnp.exp(heights), dims[dim] // parts).reshape((-1,) + (1,) * (len(dims) - dim - 1))

    level = one(*shards[0])
    for cut in shards[1:]:
        level = level * one(*cut)
    return level


def noise(stream_key, extent, scale, reach, pieces=(), held_as=jnp.bfloat16):
    array = jax.random.normal(stream_key, extent, jnp.float32) * scale
    if len(pieces) > 0:
        array = block_scale(stream_key, extent, pieces, -0.22, 0.18) * array
    return jnp.clip(array, min=-reach, max=reach).astype(held_as)


def setup_inputs(seed: int = 0) -> dict:
    streams_of = jax.random.split(jax.random.key(seed), 12)
    hidden = noise(streams_of[0], (STEPS, PROMPTS, SAMPLES, D), 1.0, 6.0, ((1, 16), (2, 16)))
    norm_gain = jnp.clip(1.0 + 0.1 * jax.random.normal(streams_of[1], (D,), jnp.float32), 0.5, 1.5)
    w_qkv = noise(streams_of[2], (D, QD + 2 * KVD), D ** -0.5, 0.078125, ((1, 16),))
    query_gain = draw_query_gain(jax.random.fold_in(streams_of[11], 71), 0)
    key_gain = jnp.clip(jnp.exp(jax.random.uniform(streams_of[4], (HD,), jnp.float32, math.log(0.5), math.log(4.0))), 0.5, 4.0)
    prompt_kv = draw_prompt_kv(jax.random.fold_in(streams_of[11], 71), 0)
    block_table = draw_block_table(jax.random.fold_in(streams_of[11], 71), 0)
    prompt_slot = jax.vmap(lambda own: jax.random.permutation(own, PROMPTS_DEV))(jax.random.split(streams_of[7], GROUPS)).reshape((GROUPS, PROMPTS_DEV)).astype(jnp.int32)
    prompt_len = draw_prompt_len(jax.random.fold_in(streams_of[11], 71), 0)
    resp_kv = draw_resp_kv(jax.random.fold_in(streams_of[11], 71), 0)
    resp_len = draw_resp_len(jax.random.fold_in(streams_of[11], 71), 0)
    return {"hidden": hidden, "norm_gain": norm_gain, "w_qkv": w_qkv, "query_gain": query_gain, "key_gain": key_gain, "prompt_kv": prompt_kv, "block_table": block_table, "prompt_slot": prompt_slot, "prompt_len": prompt_len, "resp_kv": resp_kv, "resp_len": resp_len}


def rms_scale(values_in, scale_gain):
    return values_in * lax.rsqrt(lax.optimization_barrier(jnp.mean(values_in * values_in, axis=-1, keepdims=True)) + 1e-06) * scale_gain

def rotary(values_in, positions):
    width = values_in.shape[-1]
    half_width = width // 2
    inv_freq = jnp.exp(-jnp.log(1000000.0) * jnp.arange(half_width, dtype=jnp.float32) * 2.0 / width)
    angles = positions.astype(jnp.float32)[..., None, None] * inv_freq
    cosine = jnp.cos(angles)
    sine = jnp.sin(angles)
    first = values_in[..., :half_width]
    second = values_in[..., half_width:]
    return jnp.concatenate([first * cosine - second * sine, second * cosine + first * sine], axis=-1)

def attend(queries, key_vals, valid_mask):
    feature = key_vals.shape[-1] // 2
    count, length = (key_vals.shape[0], key_vals.shape[1])
    head_dim = queries.shape[-1]
    key_part = key_vals[..., :feature].reshape(count, length, KV_HEADS, head_dim).astype(jnp.float32)
    value_part = key_vals[..., feature:].reshape(count, length, KV_HEADS, head_dim).astype(jnp.float32)
    scores = jnp.einsum('nrkgd,nlkd->nrkgl', queries.astype(jnp.float32), key_part) * head_dim ** (-0.5)
    scores = jnp.where(valid_mask[:, :, None, None, :], scores, -1e+30)
    row_max = lax.optimization_barrier(jnp.max(scores, axis=-1))
    weights = jnp.exp(scores - row_max[..., None])
    row_sum = lax.optimization_barrier(jnp.sum(weights, axis=-1))
    rounded = weights.astype(jnp.bfloat16).astype(jnp.float32)
    mixed = jnp.einsum('nrkgl,nlkd->nrkgd', rounded, value_part)
    return (row_max, row_sum, mixed)

def combine(first, second):
    max_one, sum_one, mix_one = first
    max_two, sum_two, mix_two = second
    peak = jnp.maximum(max_one, max_two)
    factor_one = jnp.exp(max_one - peak)
    factor_two = jnp.exp(max_two - peak)
    numer = mix_one * factor_one[..., None] + mix_two * factor_two[..., None]
    denom = sum_one * factor_one + sum_two * factor_two
    return (numer / denom[..., None]).astype(jnp.bfloat16)

def reference(hidden, norm_gain, w_qkv, query_gain, key_gain, prompt_kv, block_table, prompt_slot, prompt_len, resp_kv, resp_len):
    group_size = HEADS // KV_HEADS
    wide = hidden.astype(jnp.float32)
    normed = rms_scale(wide, norm_gain.astype(jnp.float32)).astype(jnp.bfloat16)
    flat_rows = normed.reshape(STEPS * PROMPTS * SAMPLES, D)
    projected = jnp.dot(flat_rows, w_qkv, preferred_element_type=jnp.float32).astype(jnp.bfloat16)
    projected = projected.reshape(STEPS, PROMPTS, SAMPLES, QD + 2 * KVD)
    lengths = prompt_len.reshape(PROMPTS)
    positions = lengths[None, :, None] + resp_len[None, :, :] + jnp.arange(STEPS, dtype=jnp.int32)[:, None, None]
    query_raw = projected[..., :QD].astype(jnp.float32).reshape(STEPS, PROMPTS, SAMPLES, HEADS, HD)
    key_raw = projected[..., QD:QD + KVD].astype(jnp.float32).reshape(STEPS, PROMPTS, SAMPLES, KV_HEADS, HD)
    value_new = projected[..., QD + KVD:]
    queries = rotary(rms_scale(query_raw, query_gain.astype(jnp.float32)), positions).astype(jnp.bfloat16)
    key_new = rotary(rms_scale(key_raw, key_gain.astype(jnp.float32)), positions).astype(jnp.bfloat16)
    new_kv = jnp.concatenate([key_new.reshape(STEPS, PROMPTS, SAMPLES, KVD), value_new], axis=-1)
    queries = queries.reshape(STEPS, PROMPTS, SAMPLES, KV_HEADS, group_size, HD).transpose(1, 2, 0, 3, 4, 5)
    new_kv = new_kv.transpose(1, 2, 0, 3)
    group_of = jnp.arange(PROMPTS, dtype=jnp.int32) // PROMPTS_DEV
    slot_flat = prompt_slot.reshape(PROMPTS).astype(jnp.int32)
    tables = block_table[group_of, slot_flat]
    page_ids = (slot_flat // OWN_DEV * (OWN_DEV * PAGES))[:, None] + tables

    def one_prompt(items):
        query_p, fresh_kv, cache_kv, cache_len, prefix_len, group_id, page_row = items
        prefix_kv = jnp.take(prompt_kv[group_id], page_row, axis=0).reshape(1, PLEN, 2 * KVD)
        prefix_mask = (jnp.arange(PLEN, dtype=jnp.int32) < prefix_len)[None, None, :]
        flat_query = query_p.reshape(1, SAMPLES * STEPS, KV_HEADS, group_size, HD)
        pre_max, pre_sum, pre_mix = attend(flat_query, prefix_kv, prefix_mask)
        prefix_stats = (pre_max.reshape(SAMPLES, STEPS, KV_HEADS, group_size), pre_sum.reshape(SAMPLES, STEPS, KV_HEADS, group_size), pre_mix.reshape(SAMPLES, STEPS, KV_HEADS, group_size, HD))
        joined = jnp.concatenate([cache_kv, fresh_kv], axis=1)
        spots = jnp.arange(RL + STEPS, dtype=jnp.int32)[None, None, :]
        step_ids = jnp.arange(STEPS, dtype=jnp.int32)[None, :, None]
        resp_mask = jnp.where(spots < RL, spots < cache_len[:, None, None], spots - RL <= step_ids)
        resp_stats = attend(query_p, joined, resp_mask)
        return combine(prefix_stats, resp_stats)
    result = lax.map(one_prompt, (queries, new_kv, resp_kv, resp_len, lengths, group_of, page_ids))
    return result.reshape(PROMPTS, SAMPLES, STEPS, QD).transpose(2, 0, 1, 3)
```

```python
import functools

import jax
import jax.numpy as jnp
import numpy as np
from jax import lax
from jax.experimental import pallas as pl
from jax.experimental.pallas import tpu as pltpu
from jax.sharding import Mesh, PartitionSpec as P

D = 5120
HD = 128
HEADS = 32
KV_HEADS = 4
GROUP = HEADS // KV_HEADS
QD = 4096
KVD = 512
STEPS = 4
SLOTS = 16
ROWS = STEPS * SLOTS
PLEN = 512
RL = 128
NEW = 16
RK = RL + NEW
SCALE = HD**-0.5
FSDP = ("yl", "z")
SAMPLE = ("yh", "x", "c")


def slot_of(j, yh, x, c):
    return ((j // 8) ^ yh) * 8 + ((x + (j // 2) % 4) % 4) * 2 + ((j % 2) ^ c)


def norm_kernel(place_ref, slots_ref, gain_ref, hidden_ref, normed_ref, perm_ref):
    row = lax.broadcasted_iota(jnp.int32, (ROWS, ROWS), 0)
    col = lax.broadcasted_iota(jnp.int32, (ROWS, ROWS), 1)
    want = slot_of(row // STEPS, place_ref[0], place_ref[1], place_ref[2])
    have = jnp.concatenate([slots_ref[...]] * STEPS, axis=1)
    hit = (want == have) & (row % STEPS == col // SLOTS)
    perm = jnp.where(hit, 1.0, 0.0).astype(jnp.bfloat16)
    perm_ref[...] = perm
    wide = hidden_ref[...].astype(jnp.float32)
    mean = jnp.mean(wide * wide, axis=-1, keepdims=True)
    normed = (wide * lax.rsqrt(mean + 1e-6) * gain_ref[...]).astype(jnp.bfloat16)
    normed_ref[...] = jnp.dot(perm, normed, preferred_element_type=jnp.float32).astype(jnp.bfloat16)


def norm_rows(place, slots, gain, hidden):
    vmem = pl.BlockSpec(memory_space=pltpu.VMEM)
    return pl.pallas_call(
        norm_kernel,
        out_shape=(
            jax.ShapeDtypeStruct((ROWS, D), jnp.bfloat16),
            jax.ShapeDtypeStruct((ROWS, ROWS), jnp.bfloat16),
        ),
        in_specs=[pl.BlockSpec(memory_space=pltpu.SMEM), vmem, vmem, vmem],
        out_specs=(vmem, vmem),
        compiler_params=pltpu.CompilerParams(vmem_limit_bytes=16 * 2**20),
        cost_estimate=pl.CostEstimate(flops=2 * ROWS * ROWS * D, bytes_accessed=4 * ROWS * D, transcendentals=0),
    )(place, slots, gain, hidden)


KSTEP = 640


def project_kernel(place_ref, rows_ref, own_ref, near_ref, far_ref, out_ref, weights, acc):
    step = pl.program_id(0)
    yl, odd = place_ref[0], place_ref[1]
    side = pl.multiple_of(odd * 64, 64)
    tail = pl.multiple_of((1 - odd) * 256, 64)

    def put(which, block):
        weights[pl.ds(pl.multiple_of(which * 256, 256), 256), :] = block[pl.ds(side, 256), :]
        weights[pl.ds(pl.multiple_of(512 + which * 64, 64), 64), :] = block[pl.ds(tail, 64), :]

    put(yl, own_ref)

    @pl.when(step < 4)
    def _():
        put(1 - yl, near_ref)

    @pl.when(step >= 4)
    def _():
        put(1 - yl, far_ref)

    @pl.when(step == 0)
    def _():
        acc[...] = jnp.zeros_like(acc)

    acc[...] += lax.dot_general(
        rows_ref[...], weights[...], (((1,), (1,)), ((), ())), preferred_element_type=jnp.float32
    )

    @pl.when(step == 7)
    def _():
        out_ref[...] = acc[...].astype(jnp.bfloat16)


def project(place, rows, own_w, near, far):
    count, width = rows.shape[0], own_w.shape[0]

    def slab(step, place_ref):
        return (0, ((step // 4) ^ place_ref[2]) * 4 + step % 4)

    return pl.pallas_call(
        project_kernel,
        out_shape=jax.ShapeDtypeStruct((count, 2 * width), jnp.bfloat16),
        grid_spec=pltpu.PrefetchScalarGridSpec(
            num_scalar_prefetch=1,
            grid=(8,),
            in_specs=[
                pl.BlockSpec((count, KSTEP), slab),
                pl.BlockSpec((width, KSTEP), slab),
                pl.BlockSpec((width, KSTEP), lambda step, place_ref: (0, jnp.minimum(step, 3))),
                pl.BlockSpec((width, KSTEP), lambda step, place_ref: (0, jnp.maximum(step - 4, 0))),
            ],
            out_specs=pl.BlockSpec((count, 2 * width), lambda step, place_ref: (0, 0)),
            scratch_shapes=[
                pltpu.VMEM((2 * width, KSTEP), jnp.bfloat16),
                pltpu.VMEM((count, 2 * width), jnp.float32),
            ],
        ),
        compiler_params=pltpu.CompilerParams(vmem_limit_bytes=24 * 2**20),
        cost_estimate=pl.CostEstimate(
            flops=4 * count * width * D, bytes_accessed=2 * D * (count + 2 * width), transcendentals=0
        ),
    )(place, rows, own_w, near, far)


PIECES = ((0, 0, 512), (1, 0, 512), (2, 0, 256), (2, 256, 256), (3, 0, 512))


def attend_kernel(*refs):
    (order, plen, rlen, cols, cosf, sinf, qgain, kgain, perm) = refs[:9]
    pages = refs[9:29]
    resp = refs[29]
    out = refs[30]
    kv, rkv, queries, mixed, sem_kv, sem_r = refs[31:]
    n = 0
    for dy in range(2):
        for dc in range(2):
            for dx, start, size in PIECES:
                j = dy * 8 + dx * 2 + dc
                pltpu.make_async_copy(pages[n], kv.at[j, pl.ds(start, size)], sem_kv.at[j]).start()
                n += 1
    for j in range(SLOTS):
        pltpu.make_async_copy(resp.at[order[j]], rkv.at[j, pl.ds(0, RL)], sem_r.at[j]).start()

    low = lax.broadcasted_iota(jnp.int32, (ROWS, HD), 1) < 64

    def head_of(hh):
        half, even, n = hh // 20, hh % 20 // 5 * 2, hh % 5
        if n < 2:
            return cols[even, :, half * 256 + n * HD : half * 256 + (n + 1) * HD].astype(jnp.float32)
        if n > 2:
            return cols[even + 1, :, half * 256 + (n - 3) * HD : half * 256 + (n - 2) * HD].astype(jnp.float32)
        left = cols[even, :, 512:640].astype(jnp.float32)
        right = cols[even + 1, :, 512:640].astype(jnp.float32)
        if half == 0:
            return jnp.where(low, left, pltpu.roll(right, 64, 1))
        return jnp.where(low, pltpu.roll(left, 64, 1), right)

    cosine, sine = cosf[...], sinf[...]

    def turned(hh, gain):
        head = head_of(hh)
        mean = jnp.mean(head * head, axis=-1, keepdims=True)
        head = head * lax.rsqrt(mean + 1e-6) * gain
        return (head * cosine + pltpu.roll(head, 64, 1) * sine).astype(jnp.bfloat16)

    fresh = [turned(HEADS + k, kgain[...]) for k in range(KV_HEADS)]
    fresh += [head_of(HEADS + KV_HEADS + k).astype(jnp.bfloat16) for k in range(KV_HEADS)]
    for k in range(2 * KV_HEADS):
        for j in range(SLOTS):
            rkv[j, RL:RK, k * HD : (k + 1) * HD] = fresh[k][j // 4 * NEW : (j // 4 + 1) * NEW]
    for h in range(HEADS):
        queries[:, h, :] = turned(h, qgain[...]).astype(jnp.float32)

    key_p = lax.broadcasted_iota(jnp.int32, (PLEN, HD), 0)
    key_r = lax.broadcasted_iota(jnp.int32, (RK, HD), 0)
    spot = key_r - RL
    step = lax.broadcasted_iota(jnp.int32, (RK, HD), 1) % 32 // GROUP
    seen = (spot >= 0) & (spot % STEPS <= step)
    turn = spot // STEPS
    across = (((1,), (1,)), ((), ()))
    down = (((0,), (0,)), ((), ()))
    factor = SCALE * 1.4426950408889634

    def one_slot(j, carry):
        pltpu.make_async_copy(kv.at[j], kv.at[j], sem_kv.at[j]).wait()
        pltpu.make_async_copy(rkv.at[j, pl.ds(0, RL)], rkv.at[j, pl.ds(0, RL)], sem_r.at[j]).wait()
        mine = queries[pl.ds(j * STEPS, STEPS)]
        zero = jnp.zeros((32, HD), jnp.float32)
        spread = []
        for k in range(KV_HEADS):
            q = mine[:, k * GROUP : (k + 1) * GROUP, :].reshape(32, HD)
            spread.append(jnp.concatenate([q if n == k else zero for n in range(KV_HEADS)], axis=1))
        q = jnp.concatenate(spread, axis=0).astype(jnp.bfloat16)
        s_p = lax.dot_general(kv[j, :, :KVD], q, across, preferred_element_type=jnp.float32)
        s_r = lax.dot_general(rkv[j, :, :KVD], q, across, preferred_element_type=jnp.float32)
        s_p = jnp.where(key_p < plen[j], s_p, -1e30)
        s_r = jnp.where((key_r < rlen[j]) | (seen & (turn == j % 4)), s_r, -1e30)
        peak = jnp.maximum(jnp.max(s_p, axis=0, keepdims=True), jnp.max(s_r, axis=0, keepdims=True))
        w_p = jnp.exp2((s_p - peak) * factor)
        w_r = jnp.exp2((s_r - peak) * factor)
        share = 1.0 / (jnp.sum(w_p, axis=0, keepdims=True) + jnp.sum(w_r, axis=0, keepdims=True))
        mix = lax.dot_general(
            (w_p * share).astype(jnp.bfloat16), kv[j, :, KVD:], down, preferred_element_type=jnp.float32
        )
        mix += lax.dot_general(
            (w_r * share).astype(jnp.bfloat16), rkv[j, :, KVD:], down, preferred_element_type=jnp.float32
        )
        for k in range(KV_HEADS):
            block = mix[k * 32 : (k + 1) * 32, k * HD : (k + 1) * HD]
            mixed[pl.ds(j * STEPS, STEPS), k * GROUP : (k + 1) * GROUP, :] = block.reshape(STEPS, GROUP, HD)
        return carry

    lax.fori_loop(0, SLOTS, one_slot, 0)
    back = perm[...]
    for h in range(HEADS):
        head = mixed[:, h, :].astype(jnp.bfloat16)
        out[:, h * HD : (h + 1) * HD] = lax.dot_general(
            back, head, (((0,), (0,)), ((), ())), preferred_element_type=jnp.float32
        ).astype(jnp.bfloat16)


def attend_all(order, plen, rlen, cols, cosf, sinf, qgain, kgain, perm, pages, resp):
    vmem = pl.BlockSpec(memory_space=pltpu.VMEM)
    smem = pl.BlockSpec(memory_space=pltpu.SMEM)
    hbm = pl.BlockSpec(memory_space=pl.ANY)
    return pl.pallas_call(
        attend_kernel,
        out_shape=jax.ShapeDtypeStruct((ROWS, QD), jnp.bfloat16),
        in_specs=[smem] * 3 + [vmem] * 6 + [hbm] * 21,
        out_specs=vmem,
        scratch_shapes=[
            pltpu.VMEM((SLOTS, PLEN, 2 * KVD), jnp.bfloat16),
            pltpu.VMEM((SLOTS, RK, 2 * KVD), jnp.bfloat16),
            pltpu.VMEM((ROWS, HEADS, HD), jnp.float32),
            pltpu.VMEM((ROWS, HEADS, HD), jnp.float32),
            pltpu.SemaphoreType.DMA((SLOTS,)),
            pltpu.SemaphoreType.DMA((SLOTS,)),
        ],
        compiler_params=pltpu.CompilerParams(vmem_limit_bytes=44 * 2**20),
        cost_estimate=pl.CostEstimate(
            flops=4 * ROWS * QD * (PLEN + RK), bytes_accessed=21 * 2**20, transcendentals=ROWS * HEADS * (PLEN + RK)
        ),
    )(order, plen, rlen, cols, cosf, sinf, qgain, kgain, perm, *pages, resp)


def shift(array, axis, size, by):
    return lax.ppermute(array, axis, [(i, (i + by) % size) for i in range(size)])


def ring(base):
    return shift(base, "x", 4, 1), shift(base, "x", 4, -1)


def far_side(up, down):
    return shift(up[:256], "x", 4, 1), shift(down[256:], "x", 4, -1)


def with_core(pieces):
    return pieces + [shift(piece, "c", 2, 1) for piece in pieces]


def swap_block(part):
    pairs = []
    for yl in range(2):
        for yh in range(2):
            for c in range(2):
                pairs.append((yl * 4 + yh * 2 + c, (1 - yl) * 4 + (yh ^ c) * 2 + c))
    return lax.ppermute(part, ("yl", "yh", "c"), pairs)


def per_device(
    hidden,
    norm_gain,
    w_qkv,
    query_gain,
    key_gain,
    prompt_kv,
    block_table,
    prompt_slot,
    prompt_len,
    resp_kv,
    resp_len,
):
    yl, z, yh, x, c = (lax.axis_index(name) for name in FSDP + SAMPLE)
    place = jnp.stack([yh, x, c]).astype(jnp.int32)
    normed, perm = norm_rows(place, prompt_slot, norm_gain.reshape(1, D), hidden.reshape(ROWS, D))
    rows = lax.all_gather(normed, "z", axis=0, tiled=True)

    own = jnp.take(prompt_kv[0], block_table[0, 0], axis=0).reshape(PLEN, 2 * KVD)
    other = shift(own, "yh", 2, 1)

    own_w = w_qkv.T
    half = D // 2
    part = lax.dynamic_slice_in_dim(own_w, c * half, half, 1)
    near = swap_block(part)
    far = shift(near, "c", 2, 1)
    up, down = ring(own)
    far_a, far_b = far_side(up, down)
    pages = with_core([own, down, far_a, far_b, up])
    up, down = ring(other)

    where = jnp.stack([yl, z % 2, c]).astype(jnp.int32)
    projected = project(where, rows, own_w, near, far)
    up, down, projected = lax.optimization_barrier((up, down, projected))
    far_a, far_b = far_side(up, down)
    pages += with_core([other, down, far_a, far_b, up])
    projected = projected.reshape(8, ROWS, 2 * own_w.shape[0])
    cols = lax.all_to_all(projected, "z", split_axis=0, concat_axis=0, tiled=True)

    want = slot_of(jnp.arange(SLOTS, dtype=jnp.int32), yh, x, c)
    hit = (prompt_slot == want[:, None]).astype(jnp.int32)
    order = jnp.sum(hit * jnp.arange(SLOTS, dtype=jnp.int32)[None, :], axis=1)
    plen = jnp.sum(hit * prompt_len, axis=1)
    rlen = jnp.sum(hit * resp_len.reshape(1, SLOTS), axis=1)
    positions = (plen + rlen)[:, None] + jnp.arange(STEPS, dtype=jnp.int32)[None, :]
    inv_freq = jnp.exp(-jnp.log(1000000.0) * jnp.arange(HD // 2, dtype=jnp.float32) * 2.0 / HD)
    angles = positions.reshape(ROWS, 1).astype(jnp.float32) * inv_freq[None, :]
    cosine, sine = jnp.cos(angles), jnp.sin(angles)
    cosf = jnp.concatenate([cosine, cosine], axis=1)
    sinf = jnp.concatenate([-sine, sine], axis=1)

    mixed = attend_all(
        order,
        plen,
        rlen,
        cols,
        cosf,
        sinf,
        query_gain.reshape(1, HD),
        key_gain.reshape(1, HD),
        perm,
        pages,
        resp_kv.reshape(SLOTS, RL, 2 * KVD),
    )
    return mixed.reshape(STEPS, SLOTS, 1, QD)


def solution(mesh):
    fine = Mesh(np.asarray(mesh.devices).reshape(2, 8, 2, 4, 2), FSDP + SAMPLE)
    placed = (
        P(None, FSDP, SAMPLE, None),
        P(),
        P(None, FSDP),
        P(),
        P(),
        P(FSDP, SAMPLE, None, None),
        P(FSDP, SAMPLE, None),
        P(FSDP, None),
        P(FSDP, None),
        P(FSDP, SAMPLE, None, None),
        P(FSDP, SAMPLE),
    )
    return jax.shard_map(
        per_device,
        mesh=fine,
        in_specs=placed,
        out_specs=P(None, FSDP, SAMPLE, None),
        check_vma=False,
    )
```

```python
import functools

import jax
import jax.numpy as jnp
import numpy as np
from jax import lax
from jax.experimental import pallas as pl
from jax.experimental.pallas import tpu as pltpu
from jax.sharding import Mesh, PartitionSpec as P

D = 5120
HD = 128
HEADS = 32
KV_HEADS = 4
GROUP = HEADS // KV_HEADS
QD = 4096
KVD = 512
STEPS = 4
SLOTS = 16
HELD = SLOTS // 2
ROWS = STEPS * SLOTS
PLEN = 512
RL = 128
NEW = 16
RK = RL + NEW
SCALE = HD**-0.5
FSDP = ("yl", "z")
SAMPLE = ("yh", "x", "c")


def slot_of(j, yh, x, c):
    return (((j // 4) ^ yh) * 4 + (x + j % 4) % 4) * 2 + c


def prepare_kernel(
    place_ref, table_ref, slots_ref, gain_ref, mine_ref, mate_ref, weights, pool, normed_ref, part_ref, pages_ref, sem
):
    depth = pl.ds(pl.multiple_of(place_ref[2] * (D // 2), 128), D // 2)
    copies = [pltpu.make_async_copy(weights.at[:, depth], part_ref, sem.at[8])]
    for n in range(8):
        copies.append(pltpu.make_async_copy(pool.at[table_ref[n]], pages_ref.at[pl.ds(n * 64, 64)], sem.at[n]))
    for copy in copies:
        copy.start()
    row = lax.broadcasted_iota(jnp.int32, (2 * ROWS, ROWS), 0)
    col = lax.broadcasted_iota(jnp.int32, (2 * ROWS, ROWS), 1)
    want = slot_of(row % ROWS // (2 * STEPS), place_ref[0], place_ref[1], row // ROWS)
    have = jnp.concatenate([slots_ref[...]] * STEPS, axis=1)
    hit = (want == have) & (row % STEPS == col // SLOTS)
    own = row // STEPS % 2 == place_ref[2]
    mine = jnp.where(hit & own, 1.0, 0.0).astype(jnp.bfloat16)
    mate = jnp.where(hit & ~own, 1.0, 0.0).astype(jnp.bfloat16)
    wide = jnp.dot(mine, mine_ref[...], preferred_element_type=jnp.float32)
    wide += jnp.dot(mate, mate_ref[...], preferred_element_type=jnp.float32)
    mean = jnp.mean(wide * wide, axis=-1, keepdims=True)
    normed_ref[...] = (wide * lax.rsqrt(mean + 1e-6) * gain_ref[...]).astype(jnp.bfloat16)
    for copy in copies:
        copy.wait()


def prepare(place, table, slots, gain, mine, mate, weights, pool):
    vmem = pl.BlockSpec(memory_space=pltpu.VMEM)
    smem = pl.BlockSpec(memory_space=pltpu.SMEM)
    hbm = pl.BlockSpec(memory_space=pl.ANY)
    return pl.pallas_call(
        prepare_kernel,
        out_shape=(
            jax.ShapeDtypeStruct((2 * ROWS, D), jnp.bfloat16),
            jax.ShapeDtypeStruct((weights.shape[0], D // 2), jnp.bfloat16),
            jax.ShapeDtypeStruct((PLEN, 2 * KVD), jnp.bfloat16),
        ),
        in_specs=[smem, smem, vmem, vmem, vmem, vmem, hbm, hbm],
        out_specs=(vmem, vmem, vmem),
        scratch_shapes=[pltpu.SemaphoreType.DMA((9,))],
        compiler_params=pltpu.CompilerParams(vmem_limit_bytes=58 * 2**20),
        cost_estimate=pl.CostEstimate(flops=8 * ROWS * ROWS * D, bytes_accessed=8 * 2**20, transcendentals=0),
    )(place, table, slots, gain, mine, mate, weights, pool)


def back_kernel(place_ref, slots_ref, kept_ref, got_ref, out_ref):
    row = lax.broadcasted_iota(jnp.int32, (ROWS, ROWS), 0)
    col = lax.broadcasted_iota(jnp.int32, (ROWS, ROWS), 1)
    have = jnp.concatenate([slots_ref[...]] * STEPS, axis=1)
    turn = (row % STEPS == col // SLOTS) & (row // STEPS % 2 == place_ref[2])
    down = (((0,), (0,)), ((), ()))
    total = jnp.zeros(out_ref.shape, jnp.float32)
    for core, ref in ((place_ref[2], kept_ref), (1 - place_ref[2], got_ref)):
        want = slot_of(row // (2 * STEPS), place_ref[0], place_ref[1], core)
        hit = jnp.where((want == have) & turn, 1.0, 0.0).astype(jnp.bfloat16)
        total += lax.dot_general(hit, ref[...], down, preferred_element_type=jnp.float32)
    out_ref[...] = total.astype(jnp.bfloat16)


def rows_back(place, slots, kept, got):
    vmem = pl.BlockSpec(memory_space=pltpu.VMEM)
    return pl.pallas_call(
        back_kernel,
        out_shape=jax.ShapeDtypeStruct((ROWS, QD), jnp.bfloat16),
        in_specs=[pl.BlockSpec(memory_space=pltpu.SMEM), vmem, vmem, vmem],
        out_specs=vmem,
        compiler_params=pltpu.CompilerParams(vmem_limit_bytes=58 * 2**20),
        cost_estimate=pl.CostEstimate(flops=4 * ROWS * ROWS * QD, bytes_accessed=4 * ROWS * QD, transcendentals=0),
    )(place, slots, kept, got)


KSTEP = 1280


def join_kernel(place_ref, own, near, far, out, sem):
    yl, odd, c = place_ref[0], place_ref[1], place_ref[2]
    head = pl.ds(pl.multiple_of(odd * 64, 64), 256)
    tail = pl.ds(pl.multiple_of((1 - odd) * 256, 64), 64)

    def to(which, size):
        base = which * 256 if size == 256 else 512 + which * 64
        return pl.ds(pl.multiple_of(base, 64), size)

    copies = []
    for rows in (head, tail):
        size = rows.size
        copies.append((own.at[rows], out.at[to(yl, size)]))
        for block, half in ((near, c), (far, 1 - c)):
            depth = pl.ds(pl.multiple_of(half * (D // 2), 128), D // 2)
            copies.append((block.at[rows], out.at[to(1 - yl, size), depth]))
    copies = [pltpu.make_async_copy(src, dst, sem.at[n]) for n, (src, dst) in enumerate(copies)]
    for copy in copies:
        copy.start()
    for copy in copies:
        copy.wait()


def join_weights(place, own_w, near, far):
    hbm = pl.BlockSpec(memory_space=pl.ANY)
    return pl.pallas_call(
        join_kernel,
        out_shape=jax.ShapeDtypeStruct((2 * own_w.shape[0], D), jnp.bfloat16),
        in_specs=[pl.BlockSpec(memory_space=pltpu.SMEM), hbm, hbm, hbm],
        out_specs=pl.BlockSpec(memory_space=pltpu.VMEM),
        scratch_shapes=[pltpu.SemaphoreType.DMA((6,))],
        compiler_params=pltpu.CompilerParams(vmem_limit_bytes=58 * 2**20),
        cost_estimate=pl.CostEstimate(flops=0, bytes_accessed=8 * D * own_w.shape[0], transcendentals=0),
    )(place, own_w, near, far)


def project_kernel(count, own_rows, *refs):
    place_ref, rows, weights, outs, total = refs[0], refs[1 : 1 + count], refs[1 + count], refs[2 + count : -1], refs[-1]
    step = pl.program_id(0)

    @pl.when(step == 0)
    def _():
        total[...] = jnp.zeros_like(total)

    both = [ref[...] for ref in rows]
    if own_rows:
        both[0] = rows[0][pl.ds(pl.multiple_of(place_ref[0] * ROWS, ROWS), ROWS)]
    total[...] += lax.dot_general(
        jnp.concatenate(both, axis=0), weights[...], (((1,), (1,)), ((), ())), preferred_element_type=jnp.float32
    )

    @pl.when(step == pl.num_programs(0) - 1)
    def _():
        base = 0
        for out in outs:
            out[...] = total[base : base + out.shape[0]].astype(jnp.bfloat16)
            base += out.shape[0]


def project(place, weights, arrays, own_rows=False):
    width = weights.shape[0]
    heights = [array.shape[0] for array in arrays]
    if own_rows:
        heights[0] = ROWS
    return pl.pallas_call(
        functools.partial(project_kernel, len(arrays), own_rows),
        out_shape=[jax.ShapeDtypeStruct((height, width), jnp.bfloat16) for height in heights],
        grid_spec=pltpu.PrefetchScalarGridSpec(
            num_scalar_prefetch=1,
            grid=(D // KSTEP,),
            in_specs=[pl.BlockSpec((array.shape[0], KSTEP), lambda step, _: (0, step)) for array in arrays]
            + [pl.BlockSpec((width, KSTEP), lambda step, _: (0, step))],
            out_specs=[pl.BlockSpec((height, width), lambda step, _: (0, 0)) for height in heights],
            scratch_shapes=[pltpu.VMEM((sum(heights), width), jnp.float32)],
        ),
        compiler_params=pltpu.CompilerParams(vmem_limit_bytes=58 * 2**20),
        cost_estimate=pl.CostEstimate(
            flops=2 * sum(heights) * width * D, bytes_accessed=2 * D * (sum(heights) + width), transcendentals=0
        ),
    )(place, *arrays, weights)


def attend_kernel(*refs):
    (order, plen, rlen, spot_z, cosf, sinf, qgain, kgain) = refs[:8]
    pages = refs[8:16]
    resp = refs[16:18]
    near_cols, far_cols = refs[18], refs[19]
    turned_cols = refs[20:26]
    out = refs[26]
    cols, kv, rkv, queries, mixed, sem_c, sem_kv, sem_r = refs[27:]
    core = spot_z[1]
    mine = pl.ds(pl.multiple_of(core * ROWS, ROWS), ROWS)
    place = spot_z[0]
    pltpu.make_async_copy(near_cols, cols.at[place], sem_c).start()
    pltpu.make_async_copy(far_cols, cols.at[(place + 4) % 8], sem_c).start()
    for k in range(3):
        ahead = (k + 1) * (1 - 2 * core)
        pltpu.make_async_copy(turned_cols[2 * k].at[mine], cols.at[(place + ahead + 8) % 8], sem_c).start()
        pltpu.make_async_copy(turned_cols[2 * k + 1].at[mine], cols.at[(place - ahead + 8) % 8], sem_c).start()
    pltpu.make_async_copy(cols, cols, sem_c).wait()
    for n in range(HELD):
        j = n // 4 * 4 + (0, 3 - 2 * core, 1 + 2 * core, 2)[n % 4]
        pltpu.make_async_copy(pages[n], kv.at[j], sem_kv.at[j]).start()
    for j in range(HELD):
        for a, sample in enumerate((core, 1 - core)):
            pltpu.make_async_copy(resp[a].at[order[j]], rkv.at[2 * j + sample, pl.ds(0, RL)], sem_r.at[j]).start()

    low = lax.broadcasted_iota(jnp.int32, (ROWS, HD), 1) < 64

    def head_of(hh):
        half, even, n = hh // 20, hh % 20 // 5 * 2, hh % 5
        if n < 2:
            return cols[even, :, half * 256 + n * HD : half * 256 + (n + 1) * HD].astype(jnp.float32)
        if n > 2:
            return cols[even + 1, :, half * 256 + (n - 3) * HD : half * 256 + (n - 2) * HD].astype(jnp.float32)
        left = cols[even, :, 512:640].astype(jnp.float32)
        right = cols[even + 1, :, 512:640].astype(jnp.float32)
        if half == 0:
            return jnp.where(low, left, pltpu.roll(right, 64, 1))
        return jnp.where(low, pltpu.roll(left, 64, 1), right)

    cosine, sine = cosf[...], sinf[...]

    def turned(hh, gain):
        head = head_of(hh)
        mean = jnp.mean(head * head, axis=-1, keepdims=True)
        head = head * lax.rsqrt(mean + 1e-6) * gain
        return (head * cosine + pltpu.roll(head, 64, 1) * sine).astype(jnp.bfloat16)

    fresh = [turned(HEADS + k, kgain[...]) for k in range(KV_HEADS)]
    fresh += [head_of(HEADS + KV_HEADS + k).astype(jnp.bfloat16) for k in range(KV_HEADS)]
    for k in range(2 * KV_HEADS):
        for n in range(SLOTS):
            rkv[n, RL:RK, k * HD : (k + 1) * HD] = fresh[k][n // 4 * NEW : (n // 4 + 1) * NEW]
    for h in range(HEADS):
        queries[h] = turned(h, qgain[...]).astype(jnp.float32)

    key_p = lax.broadcasted_iota(jnp.int32, (PLEN, 2 * HD), 0)
    key_r = lax.broadcasted_iota(jnp.int32, (RK, 2 * HD), 0)
    lane = lax.broadcasted_iota(jnp.int32, (RK, 2 * HD), 1)
    first = lane // STEPS % 2 == 0
    spot = key_r - RL
    seen = (spot >= 0) & (spot % STEPS <= lane % STEPS)
    turn = spot // STEPS
    first_row = lax.broadcasted_iota(jnp.int32, (2 * STEPS * GROUP, HD), 0) // STEPS % 2 == 0
    across = (((1,), (1,)), ((), ()))
    down = (((0,), (0,)), ((), ()))
    factor = SCALE * 1.4426950408889634
    wide = 2 * STEPS * GROUP
    zero = jnp.zeros((wide, HD), jnp.float32)

    def one_slot(j):
        rows = pl.ds(j * 2 * STEPS, 2 * STEPS)
        spread = []
        for k in range(KV_HEADS):
            q = queries[k * GROUP : (k + 1) * GROUP, rows, :].reshape(wide, HD)
            spread.append(jnp.concatenate([q if n == k else zero for n in range(KV_HEADS)], axis=1))
        q = jnp.concatenate(spread, axis=0).astype(jnp.bfloat16)
        s_p = lax.dot_general(kv[j, :, :KVD], q, across, preferred_element_type=jnp.float32)
        s_p = jnp.where(key_p < plen[j], s_p, -1e30)
        s_r = []
        for a in range(2):
            one = lax.dot_general(rkv[2 * j + a, :, :KVD], q, across, preferred_element_type=jnp.float32)
            s_r.append(jnp.where((key_r < rlen[2 * j + a]) | (seen & (turn == (2 * j + a) % 4)), one, -1e30))
        s_r = jnp.where(first, s_r[0], s_r[1])
        peak = jnp.maximum(jnp.max(s_p, axis=0, keepdims=True), jnp.max(s_r, axis=0, keepdims=True))
        w_p = jnp.exp2((s_p - peak) * factor)
        w_r = jnp.exp2((s_r - peak) * factor)
        share = 1.0 / (jnp.sum(w_p, axis=0, keepdims=True) + jnp.sum(w_r, axis=0, keepdims=True))
        w_p = (w_p * share).astype(jnp.bfloat16)
        w_r = (w_r * share).astype(jnp.bfloat16)
        mix = lax.dot_general(w_p, kv[j, :, KVD:], down, preferred_element_type=jnp.float32)
        mix_r = [
            lax.dot_general(w_r, rkv[2 * j + a, :, KVD:], down, preferred_element_type=jnp.float32) for a in range(2)
        ]
        for k in range(KV_HEADS):
            block = (slice(k * wide, (k + 1) * wide), slice(k * HD, (k + 1) * HD))
            one = mix[block] + jnp.where(first_row, mix_r[0][block], mix_r[1][block])
            mixed[k * GROUP : (k + 1) * GROUP, rows, :] = one.reshape(GROUP, 2 * STEPS, HD)

    def some_slots(i, carry):
        for n in range(BATCH):
            j = i * BATCH + n
            pltpu.make_async_copy(kv.at[j], kv.at[j], sem_kv.at[j]).wait()
            both = rkv.at[pl.ds(2 * j, 2), pl.ds(0, RL)]
            pltpu.make_async_copy(both, both, sem_r.at[j]).wait()
        for n in range(BATCH):
            one_slot(i * BATCH + n)
        return carry

    lax.fori_loop(0, HELD // BATCH, some_slots, 0)
    for h in range(HEADS):
        out[:, h * HD : (h + 1) * HD] = mixed[h].astype(jnp.bfloat16)


BATCH = 2


def attend_all(order, plen, rlen, spot_z, cosf, sinf, qgain, kgain, pages, resp, pieces):
    vmem = pl.BlockSpec(memory_space=pltpu.VMEM)
    smem = pl.BlockSpec(memory_space=pltpu.SMEM)
    hbm = pl.BlockSpec(memory_space=pl.ANY)
    return pl.pallas_call(
        attend_kernel,
        out_shape=jax.ShapeDtypeStruct((ROWS, QD), jnp.bfloat16),
        in_specs=[smem] * 4 + [vmem] * 4 + [hbm] * 18,
        out_specs=vmem,
        scratch_shapes=[
            pltpu.VMEM((8, ROWS, 640), jnp.bfloat16),
            pltpu.VMEM((HELD, PLEN, 2 * KVD), jnp.bfloat16),
            pltpu.VMEM((SLOTS, RK, 2 * KVD), jnp.bfloat16),
            pltpu.VMEM((HEADS, ROWS, HD), jnp.float32),
            pltpu.VMEM((HEADS, ROWS, HD), jnp.float32),
            pltpu.SemaphoreType.DMA,
            pltpu.SemaphoreType.DMA((HELD,)),
            pltpu.SemaphoreType.DMA((HELD,)),
        ],
        compiler_params=pltpu.CompilerParams(vmem_limit_bytes=58 * 2**20),
        cost_estimate=pl.CostEstimate(
            flops=4 * ROWS * QD * (PLEN + RK), bytes_accessed=13 * 2**20, transcendentals=ROWS * HEADS * (PLEN + RK)
        ),
    )(order, plen, rlen, spot_z, cosf, sinf, qgain, kgain, *pages, *resp, *pieces)


def shift(array, axis, size, by):
    return lax.ppermute(array, axis, [(i, (i + by) % size) for i in range(size)])


def turn(array, axis, size, by):
    pairs = []
    for n in range(size):
        for c in range(2):
            pairs.append((n * 2 + c, (n + (by if c == 0 else -by)) % size * 2 + c))
    return lax.ppermute(array, (axis, "c"), pairs)


def swap_block(part):
    pairs = []
    for yl in range(2):
        for yh in range(2):
            for c in range(2):
                pairs.append((yl * 4 + yh * 2 + c, (1 - yl) * 4 + (yh ^ c) * 2 + c))
    return lax.ppermute(part, ("yl", "yh", "c"), pairs)


def per_device(
    hidden,
    norm_gain,
    w_qkv,
    query_gain,
    key_gain,
    prompt_kv,
    block_table,
    prompt_slot,
    prompt_len,
    resp_kv,
    resp_len,
):
    yl, z, yh, x, c = (lax.axis_index(name) for name in FSDP + SAMPLE)
    place = jnp.stack([yh, x, c]).astype(jnp.int32)
    core = c.reshape(1).astype(jnp.int32)
    step = lax.optimization_barrier
    mine = hidden.reshape(ROWS, D)
    mate = shift(mine, "c", 2, 1)
    mate_len = shift(resp_len, "c", 2, 1)
    own_w = w_qkv.T
    normed, part, own = prepare(
        place, block_table[0, 0], prompt_slot, norm_gain.reshape(1, D), mine, mate, own_w, prompt_kv[0]
    )
    resp = resp_kv.reshape(SLOTS, RL, 2 * KVD)

    normed, part, own, resp, mate_len = step((normed, part, own, resp, mate_len))
    rows_1 = turn(normed, "z", 8, 1)
    near = swap_block(part)
    page_a = turn(own, "x", 4, 1)
    mate_resp = shift(resp, "c", 2, 1)
    want = slot_of(jnp.arange(HELD, dtype=jnp.int32), yh, x, c)
    hit = (prompt_slot == want[:, None]).astype(jnp.int32)
    order = jnp.sum(hit * jnp.arange(SLOTS, dtype=jnp.int32)[None, :], axis=1)
    plen = jnp.sum(hit * prompt_len, axis=1)
    lens = jnp.where(c == 0, jnp.concatenate([resp_len, mate_len], axis=1), jnp.concatenate([mate_len, resp_len], axis=1))
    rlen = jnp.sum(hit[:, :, None] * lens[None], axis=1)
    positions = (plen[:, None] + rlen)[:, :, None] + jnp.arange(STEPS, dtype=jnp.int32)
    rlen = rlen.reshape(SLOTS)
    inv_freq = jnp.exp(-jnp.log(1000000.0) * jnp.arange(HD // 2, dtype=jnp.float32) * 2.0 / HD)
    angles = positions.reshape(ROWS, 1).astype(jnp.float32) * inv_freq[None, :]
    cosine, sine = jnp.cos(angles), jnp.sin(angles)
    cosf = jnp.concatenate([cosine, cosine], axis=1)
    sinf = jnp.concatenate([-sine, sine], axis=1)

    spot = jnp.stack([z, c]).astype(jnp.int32)
    where = jnp.stack([yl, z % 2, c]).astype(jnp.int32)

    rows_1, near, page_a, mate_resp, order, plen, rlen, cosf, sinf, spot, where = step(
        (rows_1, near, page_a, mate_resp, order, plen, rlen, cosf, sinf, spot, where)
    )
    rows_2 = turn(rows_1, "z", 8, 1)
    far = shift(near, "c", 2, 1)
    page_b = turn(own, "x", 4, -1)
    other_a = shift(own[: PLEN // 2], "yh", 2, 1)
    weights = join_weights(where, own_w, near, far)
    own_cols, back_1 = project(core, weights, [normed, rows_1], True)

    rows_2, page_b, page_a, weights, back_1, other_a = step((rows_2, page_b, page_a, weights, back_1, other_a))
    other_b = shift(own[PLEN // 2 :], "yh", 2, 1)
    rows_3 = turn(rows_2, "z", 8, 1)
    page_far = turn(page_a, "x", 4, 1)
    cols_1 = turn(back_1, "z", 8, -1)
    (back_2,) = project(core, weights, [rows_2])

    rows_3, page_far, other_b, back_2, cols_1 = step((rows_3, page_far, other_b, back_2, cols_1))
    other = jnp.concatenate([other_a, other_b], axis=0)
    rows_4 = turn(lax.dynamic_slice_in_dim(rows_3, c * ROWS, ROWS, 0), "z", 8, 1)
    page_c = turn(other, "x", 4, 1)
    page_d = turn(other, "x", 4, -1)
    page_e = shift(page_far, "yh", 2, 1)
    cols_2 = turn(back_2, "z", 8, -2)

    back_3, back_4 = project(core, weights, [rows_3, rows_4])
    cols_3 = turn(back_3, "z", 8, -3)
    cols_4 = turn(back_4, "z", 8, -4)
    turned = []
    for cols in (cols_1, cols_2, cols_3):
        turned += [cols, shift(cols, "c", 2, 1)]

    kept = attend_all(
        order,
        plen,
        rlen,
        spot,
        cosf,
        sinf,
        query_gain.reshape(1, HD),
        key_gain.reshape(1, HD),
        [own, page_a, page_b, page_far, other, page_c, page_d, page_e],
        (resp, mate_resp),
        [own_cols, cols_4] + turned,
    )
    got = shift(kept, "c", 2, 1)
    return rows_back(place, prompt_slot, kept, got).reshape(STEPS, SLOTS, 1, QD)


def solution(mesh):
    fine = Mesh(np.asarray(mesh.devices).reshape(2, 8, 2, 4, 2), FSDP + SAMPLE)
    placed = (
        P(None, FSDP, SAMPLE, None),
        P(),
        P(None, FSDP),
        P(),
        P(),
        P(FSDP, SAMPLE, None, None),
        P(FSDP, SAMPLE, None),
        P(FSDP, None),
        P(FSDP, None),
        P(FSDP, SAMPLE, None, None),
        P(FSDP, SAMPLE),
    )
    return jax.shard_map(
        per_device,
        mesh=fine,
        in_specs=placed,
        out_specs=P(None, FSDP, SAMPLE, None),
        check_vma=False,
    )
```

```python
import functools

import jax
import jax.numpy as jnp
import numpy as np
from jax import lax
from jax.experimental import pallas as pl
from jax.experimental.pallas import tpu as pltpu
from jax.sharding import Mesh, PartitionSpec as P

D = 5120
HD = 128
HEADS = 32
KV_HEADS = 4
GROUP = HEADS // KV_HEADS
QD = 4096
KVD = 512
STEPS = 4
SLOTS = 16
HELD = SLOTS // 2
ROWS = STEPS * SLOTS
PLEN = 512
RL = 128
NEW = 16
RK = RL + NEW
SCALE = HD**-0.5
FSDP = ("yl", "z")
SAMPLE = ("yh", "x", "c")


def slot_of(j, yh, x, c):
    return (((j // 4) ^ yh) * 4 + (x + j % 4) % 4) * 2 + c


def prepare_kernel(
    place_ref, table_ref, slots_ref, gain_ref, mine_ref, mate_ref, weights, pool, normed_ref, part_ref, pages_ref, sem
):
    depth = pl.ds(pl.multiple_of(place_ref[2] * (D // 2), 128), D // 2)
    copies = [pltpu.make_async_copy(weights.at[:, depth], part_ref, sem.at[8])]
    for n in range(8):
        copies.append(pltpu.make_async_copy(pool.at[table_ref[n]], pages_ref.at[pl.ds(n * 64, 64)], sem.at[n]))
    for copy in copies:
        copy.start()
    row = lax.broadcasted_iota(jnp.int32, (2 * ROWS, ROWS), 0)
    col = lax.broadcasted_iota(jnp.int32, (2 * ROWS, ROWS), 1)
    want = slot_of(row % ROWS // (2 * STEPS), place_ref[0], place_ref[1], row // ROWS)
    have = jnp.concatenate([slots_ref[...]] * STEPS, axis=1)
    hit = (want == have) & (row % STEPS == col // SLOTS)
    own = row // STEPS % 2 == place_ref[2]
    pick = jnp.concatenate([jnp.where(hit & own, 1.0, 0.0), jnp.where(hit & ~own, 1.0, 0.0)], axis=1)
    both = jnp.concatenate([mine_ref[...], mate_ref[...]], axis=0)
    wide = jnp.dot(pick.astype(jnp.bfloat16), both, preferred_element_type=jnp.float32)
    mean = jnp.mean(wide * wide, axis=-1, keepdims=True)
    normed_ref[...] = (wide * lax.rsqrt(mean + 1e-6) * gain_ref[...]).astype(jnp.bfloat16)
    for copy in copies:
        copy.wait()


def prepare(place, table, slots, gain, mine, mate, weights, pool):
    vmem = pl.BlockSpec(memory_space=pltpu.VMEM)
    smem = pl.BlockSpec(memory_space=pltpu.SMEM)
    hbm = pl.BlockSpec(memory_space=pl.ANY)
    return pl.pallas_call(
        prepare_kernel,
        out_shape=(
            jax.ShapeDtypeStruct((2 * ROWS, D), jnp.bfloat16),
            jax.ShapeDtypeStruct((weights.shape[0], D // 2), jnp.bfloat16),
            jax.ShapeDtypeStruct((PLEN, 2 * KVD), jnp.bfloat16),
        ),
        in_specs=[smem, smem, vmem, vmem, vmem, vmem, hbm, hbm],
        out_specs=(vmem, vmem, vmem),
        scratch_shapes=[pltpu.SemaphoreType.DMA((9,))],
        compiler_params=pltpu.CompilerParams(vmem_limit_bytes=62 * 2**20),
        cost_estimate=pl.CostEstimate(flops=8 * ROWS * ROWS * D, bytes_accessed=8 * 2**20, transcendentals=0),
    )(place, table, slots, gain, mine, mate, weights, pool)


def back_kernel(place_ref, slots_ref, kept_ref, got_ref, out_ref):
    row = lax.broadcasted_iota(jnp.int32, (ROWS, ROWS), 0)
    col = lax.broadcasted_iota(jnp.int32, (ROWS, ROWS), 1)
    have = jnp.concatenate([slots_ref[...]] * STEPS, axis=1)
    turn = (row % STEPS == col // SLOTS) & (row // STEPS % 2 == place_ref[2])
    down = (((0,), (0,)), ((), ()))
    total = jnp.zeros(out_ref.shape, jnp.float32)
    for core, ref in ((place_ref[2], kept_ref), (1 - place_ref[2], got_ref)):
        want = slot_of(row // (2 * STEPS), place_ref[0], place_ref[1], core)
        hit = jnp.where((want == have) & turn, 1.0, 0.0).astype(jnp.bfloat16)
        total += lax.dot_general(hit, ref[...], down, preferred_element_type=jnp.float32)
    out_ref[...] = total.astype(jnp.bfloat16)


def rows_back(place, slots, kept, got):
    vmem = pl.BlockSpec(memory_space=pltpu.VMEM)
    return pl.pallas_call(
        back_kernel,
        out_shape=jax.ShapeDtypeStruct((ROWS, QD), jnp.bfloat16),
        in_specs=[pl.BlockSpec(memory_space=pltpu.SMEM), vmem, vmem, vmem],
        out_specs=vmem,
        compiler_params=pltpu.CompilerParams(vmem_limit_bytes=62 * 2**20),
        cost_estimate=pl.CostEstimate(flops=4 * ROWS * ROWS * QD, bytes_accessed=4 * ROWS * QD, transcendentals=0),
    )(place, slots, kept, got)


KSTEP = 2560


def join_kernel(place_ref, own, near, far, out, sem):
    c, yl, odd = place_ref[2], place_ref[3], place_ref[4]
    head = pl.ds(pl.multiple_of(odd * 64, 64), 256)
    tail = pl.ds(pl.multiple_of((1 - odd) * 256, 64), 64)

    def to(which, size):
        base = which * 256 if size == 256 else 512 + which * 64
        return pl.ds(pl.multiple_of(base, 64), size)

    copies = []
    for rows in (head, tail):
        size = rows.size
        copies.append((own.at[rows], out.at[to(yl, size)]))
        for block, half in ((near, c), (far, 1 - c)):
            depth = pl.ds(pl.multiple_of(half * (D // 2), 128), D // 2)
            copies.append((block.at[rows], out.at[to(1 - yl, size), depth]))
    copies = [pltpu.make_async_copy(src, dst, sem.at[n]) for n, (src, dst) in enumerate(copies)]
    for copy in copies:
        copy.start()
    for copy in copies:
        copy.wait()


def join_weights(place, own_w, near, far):
    hbm = pl.BlockSpec(memory_space=pl.ANY)
    return pl.pallas_call(
        join_kernel,
        out_shape=jax.ShapeDtypeStruct((2 * own_w.shape[0], D), jnp.bfloat16),
        in_specs=[pl.BlockSpec(memory_space=pltpu.SMEM), hbm, hbm, hbm],
        out_specs=pl.BlockSpec(memory_space=pltpu.VMEM),
        scratch_shapes=[pltpu.SemaphoreType.DMA((6,))],
        compiler_params=pltpu.CompilerParams(vmem_limit_bytes=62 * 2**20),
        cost_estimate=pl.CostEstimate(flops=0, bytes_accessed=8 * D * own_w.shape[0], transcendentals=0),
    )(place, own_w, near, far)


def project_kernel(count, own_rows, *refs):
    place_ref, rows, weights, outs, total = refs[0], refs[1 : 1 + count], refs[1 + count], refs[2 + count : -1], refs[-1]
    step = pl.program_id(0)

    @pl.when(step == 0)
    def _():
        total[...] = jnp.zeros_like(total)

    both = [ref[...] for ref in rows]
    if own_rows:
        both[0] = rows[0][pl.ds(pl.multiple_of(place_ref[2] * ROWS, ROWS), ROWS)]
    total[...] += lax.dot_general(
        jnp.concatenate(both, axis=0), weights[...], (((1,), (1,)), ((), ())), preferred_element_type=jnp.float32
    )

    @pl.when(step == pl.num_programs(0) - 1)
    def _():
        base = 0
        for out in outs:
            out[...] = total[base : base + out.shape[0]].astype(jnp.bfloat16)
            base += out.shape[0]


def project(place, weights, arrays, own_rows=False):
    width = weights.shape[0]
    heights = [array.shape[0] for array in arrays]
    if own_rows:
        heights[0] = ROWS
    return pl.pallas_call(
        functools.partial(project_kernel, len(arrays), own_rows),
        out_shape=[jax.ShapeDtypeStruct((height, width), jnp.bfloat16) for height in heights],
        grid_spec=pltpu.PrefetchScalarGridSpec(
            num_scalar_prefetch=1,
            grid=(D // KSTEP,),
            in_specs=[pl.BlockSpec((array.shape[0], KSTEP), lambda step, _: (0, step)) for array in arrays]
            + [pl.BlockSpec((width, KSTEP), lambda step, _: (0, step))],
            out_specs=[pl.BlockSpec((height, width), lambda step, _: (0, 0)) for height in heights],
            scratch_shapes=[pltpu.VMEM((sum(heights), width), jnp.float32)],
        ),
        compiler_params=pltpu.CompilerParams(vmem_limit_bytes=62 * 2**20),
        cost_estimate=pl.CostEstimate(
            flops=2 * sum(heights) * width * D, bytes_accessed=2 * D * (sum(heights) + width), transcendentals=0
        ),
    )(place, *arrays, weights)


def attend_kernel(*refs):
    (order, plen, rlen, spot_z, cosf, sinf, qgain, kgain) = refs[:8]
    pages = refs[8:16]
    resp = refs[16:18]
    near_cols, far_cols = refs[18], refs[19]
    turned_cols = refs[20:26]
    out = refs[26]
    cols, kv, rkv, queries, mixed, sem_c, sem_kv, sem_r = refs[27:]
    core = spot_z[2]
    mine = pl.ds(pl.multiple_of(core * ROWS, ROWS), ROWS)
    place = spot_z[5]
    pltpu.make_async_copy(near_cols, cols.at[place], sem_c).start()
    pltpu.make_async_copy(far_cols, cols.at[(place + 4) % 8], sem_c).start()
    for k in range(3):
        ahead = (k + 1) * (1 - 2 * core)
        pltpu.make_async_copy(turned_cols[2 * k].at[mine], cols.at[(place + ahead + 8) % 8], sem_c).start()
        pltpu.make_async_copy(turned_cols[2 * k + 1].at[mine], cols.at[(place - ahead + 8) % 8], sem_c).start()
    pltpu.make_async_copy(cols, cols, sem_c).wait()
    for n in range(HELD):
        j = n // 4 * 4 + (0, 3 - 2 * core, 1 + 2 * core, 2)[n % 4]
        pltpu.make_async_copy(pages[n], kv.at[j], sem_kv.at[j]).start()
    for j in range(HELD):
        for a, sample in enumerate((core, 1 - core)):
            pltpu.make_async_copy(resp[a].at[order[j]], rkv.at[2 * j + sample, pl.ds(0, RL)], sem_r.at[j]).start()

    low = lax.broadcasted_iota(jnp.int32, (ROWS, HD), 1) < 64

    def head_of(hh):
        half, even, n = hh // 20, hh % 20 // 5 * 2, hh % 5
        if n < 2:
            return cols[even, :, half * 256 + n * HD : half * 256 + (n + 1) * HD].astype(jnp.float32)
        if n > 2:
            return cols[even + 1, :, half * 256 + (n - 3) * HD : half * 256 + (n - 2) * HD].astype(jnp.float32)
        left = cols[even, :, 512:640].astype(jnp.float32)
        right = cols[even + 1, :, 512:640].astype(jnp.float32)
        if half == 0:
            return jnp.where(low, left, pltpu.roll(right, 64, 1))
        return jnp.where(low, pltpu.roll(left, 64, 1), right)

    cosine, sine = cosf[...], sinf[...]

    def turned(hh, gain):
        head = head_of(hh)
        mean = jnp.mean(head * head, axis=-1, keepdims=True)
        head = head * lax.rsqrt(mean + 1e-6) * gain
        return (head * cosine + pltpu.roll(head, 64, 1) * sine).astype(jnp.bfloat16)

    fresh = [turned(HEADS + k, kgain[...]) for k in range(KV_HEADS)]
    fresh += [head_of(HEADS + KV_HEADS + k).astype(jnp.bfloat16) for k in range(KV_HEADS)]
    for k in range(2 * KV_HEADS):
        for n in range(SLOTS):
            rkv[n, RL:RK, k * HD : (k + 1) * HD] = fresh[k][n // 4 * NEW : (n // 4 + 1) * NEW]
    for h in range(HEADS):
        queries[h] = turned(h, qgain[...]).astype(jnp.float32)

    key_p = lax.broadcasted_iota(jnp.int32, (PLEN, 2 * HD), 0)
    key_r = lax.broadcasted_iota(jnp.int32, (RK, 2 * HD), 0)
    lane = lax.broadcasted_iota(jnp.int32, (RK, 2 * HD), 1)
    first = lane // STEPS % 2 == 0
    spot = key_r - RL
    seen = (spot >= 0) & (spot % STEPS <= lane % STEPS)
    turn = spot // STEPS
    first_row = lax.broadcasted_iota(jnp.int32, (2 * STEPS * GROUP, HD), 0) // STEPS % 2 == 0
    across = (((1,), (1,)), ((), ()))
    down = (((0,), (0,)), ((), ()))
    factor = SCALE * 1.4426950408889634
    wide = 2 * STEPS * GROUP
    zero = jnp.zeros((wide, HD), jnp.float32)

    def one_slot(j):
        rows = pl.ds(j * 2 * STEPS, 2 * STEPS)
        spread = []
        for k in range(KV_HEADS):
            q = queries[k * GROUP : (k + 1) * GROUP, rows, :].reshape(wide, HD)
            spread.append(jnp.concatenate([q if n == k else zero for n in range(KV_HEADS)], axis=1))
        q = jnp.concatenate(spread, axis=0).astype(jnp.bfloat16)
        s_p = lax.dot_general(kv[j, :, :KVD], q, across, preferred_element_type=jnp.float32)
        s_p = jnp.where(key_p < plen[j], s_p, -1e30)
        s_r = []
        for a in range(2):
            one = lax.dot_general(rkv[2 * j + a, :, :KVD], q, across, preferred_element_type=jnp.float32)
            s_r.append(jnp.where((key_r < rlen[2 * j + a]) | (seen & (turn == (2 * j + a) % 4)), one, -1e30))
        s_r = jnp.where(first, s_r[0], s_r[1])
        peak = jnp.maximum(jnp.max(s_p, axis=0, keepdims=True), jnp.max(s_r, axis=0, keepdims=True))
        w_p = jnp.exp2((s_p - peak) * factor)
        w_r = jnp.exp2((s_r - peak) * factor)
        share = 1.0 / (jnp.sum(w_p, axis=0, keepdims=True) + jnp.sum(w_r, axis=0, keepdims=True))
        w_p = (w_p * share).astype(jnp.bfloat16)
        w_r = (w_r * share).astype(jnp.bfloat16)
        mix = lax.dot_general(w_p, kv[j, :, KVD:], down, preferred_element_type=jnp.float32)
        mix_r = [
            lax.dot_general(w_r, rkv[2 * j + a, :, KVD:], down, preferred_element_type=jnp.float32) for a in range(2)
        ]
        for k in range(KV_HEADS):
            block = (slice(k * wide, (k + 1) * wide), slice(k * HD, (k + 1) * HD))
            one = mix[block] + jnp.where(first_row, mix_r[0][block], mix_r[1][block])
            mixed[k * GROUP : (k + 1) * GROUP, rows, :] = one.reshape(GROUP, 2 * STEPS, HD)

    def some_slots(i, carry):
        for n in range(BATCH):
            j = i * BATCH + n
            pltpu.make_async_copy(kv.at[j], kv.at[j], sem_kv.at[j]).wait()
            both = rkv.at[pl.ds(2 * j, 2), pl.ds(0, RL)]
            pltpu.make_async_copy(both, both, sem_r.at[j]).wait()
        for n in range(BATCH):
            one_slot(i * BATCH + n)
        return carry

    lax.fori_loop(0, HELD // BATCH, some_slots, 0)
    for h in range(HEADS):
        out[:, h * HD : (h + 1) * HD] = mixed[h].astype(jnp.bfloat16)


BATCH = 2


def attend_all(order, plen, rlen, spot_z, cosf, sinf, qgain, kgain, pages, resp, pieces):
    vmem = pl.BlockSpec(memory_space=pltpu.VMEM)
    smem = pl.BlockSpec(memory_space=pltpu.SMEM)
    hbm = pl.BlockSpec(memory_space=pl.ANY)
    return pl.pallas_call(
        attend_kernel,
        out_shape=jax.ShapeDtypeStruct((ROWS, QD), jnp.bfloat16),
        in_specs=[smem] * 4 + [vmem] * 4 + [hbm] * 18,
        out_specs=vmem,
        scratch_shapes=[
            pltpu.VMEM((8, ROWS, 640), jnp.bfloat16),
            pltpu.VMEM((HELD, PLEN, 2 * KVD), jnp.bfloat16),
            pltpu.VMEM((SLOTS, RK, 2 * KVD), jnp.bfloat16),
            pltpu.VMEM((HEADS, ROWS, HD), jnp.float32),
            pltpu.VMEM((HEADS, ROWS, HD), jnp.float32),
            pltpu.SemaphoreType.DMA,
            pltpu.SemaphoreType.DMA((HELD,)),
            pltpu.SemaphoreType.DMA((HELD,)),
        ],
        compiler_params=pltpu.CompilerParams(vmem_limit_bytes=62 * 2**20),
        cost_estimate=pl.CostEstimate(
            flops=4 * ROWS * QD * (PLEN + RK), bytes_accessed=13 * 2**20, transcendentals=ROWS * HEADS * (PLEN + RK)
        ),
    )(order, plen, rlen, spot_z, cosf, sinf, qgain, kgain, *pages, *resp, *pieces)


def shift(array, axis, size, by):
    return lax.ppermute(array, axis, [(i, (i + by) % size) for i in range(size)])


def turn(array, axis, size, by):
    pairs = []
    for n in range(size):
        for c in range(2):
            pairs.append((n * 2 + c, (n + (by if c == 0 else -by)) % size * 2 + c))
    return lax.ppermute(array, (axis, "c"), pairs)


def swap_block(part):
    pairs = []
    for yl in range(2):
        for yh in range(2):
            for c in range(2):
                pairs.append((yl * 4 + yh * 2 + c, (1 - yl) * 4 + (yh ^ c) * 2 + c))
    return lax.ppermute(part, ("yl", "yh", "c"), pairs)


def per_device(
    hidden,
    norm_gain,
    w_qkv,
    query_gain,
    key_gain,
    prompt_kv,
    block_table,
    prompt_slot,
    prompt_len,
    resp_kv,
    resp_len,
):
    yl, z, yh, x, c = (lax.axis_index(name) for name in FSDP + SAMPLE)
    place = jnp.stack([yh, x, c, yl, z % 2, z]).astype(jnp.int32)
    step = lax.optimization_barrier
    mine = hidden.reshape(ROWS, D)
    mate = shift(mine, "c", 2, 1)
    mate_len = shift(resp_len, "c", 2, 1)
    own_w = w_qkv.T
    normed, part, own = prepare(
        place, block_table[0, 0], prompt_slot, norm_gain.reshape(1, D), mine, mate, own_w, prompt_kv[0]
    )
    resp = resp_kv.reshape(SLOTS, RL, 2 * KVD)

    normed, part, own, resp, mate_len = step((normed, part, own, resp, mate_len))
    rows_1 = turn(normed, "z", 8, 1)
    near = swap_block(part)
    page_a = turn(own, "x", 4, 1)
    mate_resp = shift(resp, "c", 2, 1)

    rows_1, near, page_a, mate_resp = step((rows_1, near, page_a, mate_resp))
    rows_2 = turn(rows_1, "z", 8, 1)
    far = shift(near, "c", 2, 1)
    page_far = turn(page_a, "x", 4, 1)
    other_a = shift(own[: PLEN // 2], "yh", 2, 1)
    weights = join_weights(place, own_w, near, far)
    own_cols, back_1 = project(place, weights, [normed, rows_1], True)

    rows_2, page_far, weights, back_1, other_a, slots, own = step(
        (rows_2, page_far, weights, back_1, other_a, prompt_slot, own)
    )
    other_b = shift(own[PLEN // 2 :], "yh", 2, 1)
    rows_3 = turn(rows_2, "z", 8, 1)
    page_b = turn(own, "x", 4, -1)
    page_e = shift(page_far, "yh", 2, 1)
    cols_1 = turn(back_1, "z", 8, -1)
    (back_2,) = project(place, weights, [rows_2])

    want = slot_of(jnp.arange(HELD, dtype=jnp.int32), yh, x, c)
    hit = (slots == want[:, None]).astype(jnp.int32)
    order = jnp.sum(hit * jnp.arange(SLOTS, dtype=jnp.int32)[None, :], axis=1)
    plen = jnp.sum(hit * prompt_len, axis=1)
    lens = jnp.where(c == 0, jnp.concatenate([resp_len, mate_len], axis=1), jnp.concatenate([mate_len, resp_len], axis=1))
    rlen = jnp.sum(hit[:, :, None] * lens[None], axis=1)
    positions = (plen[:, None] + rlen)[:, :, None] + jnp.arange(STEPS, dtype=jnp.int32)
    rlen = rlen.reshape(SLOTS)
    inv_freq = jnp.exp(-jnp.log(1000000.0) * jnp.arange(HD // 2, dtype=jnp.float32) * 2.0 / HD)
    angles = positions.reshape(ROWS, 1).astype(jnp.float32) * inv_freq[None, :]
    cosine, sine = jnp.cos(angles), jnp.sin(angles)
    cosf = jnp.concatenate([cosine, cosine], axis=1)
    sinf = jnp.concatenate([-sine, sine], axis=1)


    rows_3, page_b, other_b, back_2, cols_1, order, plen, rlen, cosf, sinf = step(
        (rows_3, page_b, other_b, back_2, cols_1, order, plen, rlen, cosf, sinf)
    )
    other = jnp.concatenate([other_a, other_b], axis=0)
    rows_4 = turn(lax.dynamic_slice_in_dim(rows_3, c * ROWS, ROWS, 0), "z", 8, 1)
    page_c = turn(other, "x", 4, 1)
    page_d = turn(other, "x", 4, -1)
    cols_2 = turn(back_2, "z", 8, -2)

    back_3, back_4 = project(place, weights, [rows_3, rows_4])
    cols_3 = turn(back_3, "z", 8, -3)
    cols_4 = turn(back_4, "z", 8, -4)
    cols_3, cols_4 = step((cols_3, cols_4))
    turned = []
    for cols in (cols_1, cols_2, cols_3):
        turned += [cols, shift(cols, "c", 2, 1)]

    kept = attend_all(
        order,
        plen,
        rlen,
        place,
        cosf,
        sinf,
        query_gain.reshape(1, HD),
        key_gain.reshape(1, HD),
        [own, page_a, page_b, page_far, other, page_c, page_d, page_e],
        (resp, mate_resp),
        [own_cols, cols_4] + turned,
    )
    got = shift(kept, "c", 2, 1)
    return rows_back(place, prompt_slot, kept, got).reshape(STEPS, SLOTS, 1, QD)


def solution(mesh):
    fine = Mesh(np.asarray(mesh.devices).reshape(2, 8, 2, 4, 2), FSDP + SAMPLE)
    placed = (
        P(None, FSDP, SAMPLE, None),
        P(),
        P(None, FSDP),
        P(),
        P(),
        P(FSDP, SAMPLE, None, None),
        P(FSDP, SAMPLE, None),
        P(FSDP, None),
        P(FSDP, None),
        P(FSDP, SAMPLE, None, None),
        P(FSDP, SAMPLE),
    )
    return jax.shard_map(
        per_device,
        mesh=fine,
        in_specs=placed,
        out_specs=P(None, FSDP, SAMPLE, None),
        check_vma=False,
    )
```

```python
import functools

import jax
import jax.numpy as jnp
import numpy as np
from jax import lax
from jax.experimental import pallas as pl
from jax.experimental.pallas import tpu as pltpu
from jax.sharding import Mesh, PartitionSpec as P

D = 5120
HD = 128
HEADS = 32
KV_HEADS = 4
GROUP = HEADS // KV_HEADS
QD = 4096
KVD = 512
STEPS = 4
SLOTS = 16
HELD = SLOTS // 2
ROWS = STEPS * SLOTS
PLEN = 512
RL = 128
NEW = 16
RK = RL + NEW
SCALE = HD**-0.5
FSDP = ("yl", "z")
SAMPLE = ("yh", "x", "c")


def slot_of(j, yh, x, c):
    return (((j // 4) ^ yh) * 4 + (x + j % 4) % 4) * 2 + c


def prepare_kernel(
    place_ref, table_ref, slots_ref, gain_ref, mine_ref, mate_ref, weights, pool, normed_ref, part_ref, pages_ref, sem
):
    depth = pl.ds(pl.multiple_of(place_ref[2] * (D // 2), 128), D // 2)
    copies = [pltpu.make_async_copy(weights.at[:, depth], part_ref, sem.at[8])]
    for n in range(8):
        copies.append(pltpu.make_async_copy(pool.at[table_ref[n]], pages_ref.at[pl.ds(n * 64, 64)], sem.at[n]))
    for copy in copies:
        copy.start()
    row = lax.broadcasted_iota(jnp.int32, (2 * ROWS, ROWS), 0)
    col = lax.broadcasted_iota(jnp.int32, (2 * ROWS, ROWS), 1)
    want = slot_of(row % ROWS // (2 * STEPS), place_ref[0], place_ref[1], row // ROWS)
    have = jnp.concatenate([slots_ref[...]] * STEPS, axis=1)
    hit = (want == have) & (row % STEPS == col // SLOTS)
    own = row // STEPS % 2 == place_ref[2]
    pick = jnp.concatenate([jnp.where(hit & own, 1.0, 0.0), jnp.where(hit & ~own, 1.0, 0.0)], axis=1)
    both = jnp.concatenate([mine_ref[...], mate_ref[...]], axis=0)
    wide = jnp.dot(pick.astype(jnp.bfloat16), both, preferred_element_type=jnp.float32)
    mean = jnp.mean(wide * wide, axis=-1, keepdims=True)
    normed_ref[...] = (wide * lax.rsqrt(mean + 1e-6) * gain_ref[...]).astype(jnp.bfloat16)
    for copy in copies:
        copy.wait()


def prepare(place, table, slots, gain, mine, mate, weights, pool):
    vmem = pl.BlockSpec(memory_space=pltpu.VMEM)
    smem = pl.BlockSpec(memory_space=pltpu.SMEM)
    hbm = pl.BlockSpec(memory_space=pl.ANY)
    return pl.pallas_call(
        prepare_kernel,
        out_shape=(
            jax.ShapeDtypeStruct((2 * ROWS, D), jnp.bfloat16),
            jax.ShapeDtypeStruct((weights.shape[0], D // 2), jnp.bfloat16),
            jax.ShapeDtypeStruct((PLEN, 2 * KVD), jnp.bfloat16),
        ),
        in_specs=[smem, smem, vmem, vmem, vmem, vmem, hbm, hbm],
        out_specs=(vmem, vmem, vmem),
        scratch_shapes=[pltpu.SemaphoreType.DMA((9,))],
        compiler_params=pltpu.CompilerParams(vmem_limit_bytes=255 * 2**18),
        cost_estimate=pl.CostEstimate(flops=8 * ROWS * ROWS * D, bytes_accessed=8 * 2**20, transcendentals=0),
    )(place, table, slots, gain, mine, mate, weights, pool)


def back_kernel(place_ref, slots_ref, kept_ref, got_ref, out_ref):
    row = lax.broadcasted_iota(jnp.int32, (ROWS, ROWS), 0)
    col = lax.broadcasted_iota(jnp.int32, (ROWS, ROWS), 1)
    have = jnp.concatenate([slots_ref[...]] * STEPS, axis=1)
    turn = (row % STEPS == col // SLOTS) & (row // STEPS % 2 == place_ref[2])
    down = (((0,), (0,)), ((), ()))
    total = jnp.zeros(out_ref.shape, jnp.float32)
    for core, ref in ((place_ref[2], kept_ref), (1 - place_ref[2], got_ref)):
        want = slot_of(row // (2 * STEPS), place_ref[0], place_ref[1], core)
        hit = jnp.where((want == have) & turn, 1.0, 0.0).astype(jnp.bfloat16)
        total += lax.dot_general(hit, ref[...], down, preferred_element_type=jnp.float32)
    out_ref[...] = total.astype(jnp.bfloat16)


def rows_back(place, slots, kept, got):
    vmem = pl.BlockSpec(memory_space=pltpu.VMEM)
    return pl.pallas_call(
        back_kernel,
        out_shape=jax.ShapeDtypeStruct((ROWS, QD), jnp.bfloat16),
        in_specs=[pl.BlockSpec(memory_space=pltpu.SMEM), vmem, vmem, vmem],
        out_specs=vmem,
        compiler_params=pltpu.CompilerParams(vmem_limit_bytes=255 * 2**18),
        cost_estimate=pl.CostEstimate(flops=4 * ROWS * ROWS * QD, bytes_accessed=4 * ROWS * QD, transcendentals=0),
    )(place, slots, kept, got)


KSTEP = 2560


def join_kernel(place_ref, own, near, far, out, sem):
    c, yl, odd = place_ref[2], place_ref[3], place_ref[4]
    head = pl.ds(pl.multiple_of(odd * 64, 64), 256)
    tail = pl.ds(pl.multiple_of((1 - odd) * 256, 64), 64)

    def to(which, size):
        base = which * 256 if size == 256 else 512 + which * 64
        return pl.ds(pl.multiple_of(base, 64), size)

    copies = []
    for rows in (head, tail):
        size = rows.size
        copies.append((own.at[rows], out.at[to(yl, size)]))
        for block, half in ((near, c), (far, 1 - c)):
            depth = pl.ds(pl.multiple_of(half * (D // 2), 128), D // 2)
            copies.append((block.at[rows], out.at[to(1 - yl, size), depth]))
    copies = [pltpu.make_async_copy(src, dst, sem.at[n]) for n, (src, dst) in enumerate(copies)]
    for copy in copies:
        copy.start()
    for copy in copies:
        copy.wait()


def join_weights(place, own_w, near, far):
    hbm = pl.BlockSpec(memory_space=pl.ANY)
    return pl.pallas_call(
        join_kernel,
        out_shape=jax.ShapeDtypeStruct((2 * own_w.shape[0], D), jnp.bfloat16),
        in_specs=[pl.BlockSpec(memory_space=pltpu.SMEM), hbm, hbm, hbm],
        out_specs=pl.BlockSpec(memory_space=pltpu.VMEM),
        scratch_shapes=[pltpu.SemaphoreType.DMA((6,))],
        compiler_params=pltpu.CompilerParams(vmem_limit_bytes=255 * 2**18),
        cost_estimate=pl.CostEstimate(flops=0, bytes_accessed=8 * D * own_w.shape[0], transcendentals=0),
    )(place, own_w, near, far)


def project_kernel(count, own_rows, *refs):
    place_ref, rows, weights, outs, total = refs[0], refs[1 : 1 + count], refs[1 + count], refs[2 + count : -1], refs[-1]
    step = pl.program_id(0)

    @pl.when(step == 0)
    def _():
        total[...] = jnp.zeros_like(total)

    both = [ref[...] for ref in rows]
    if own_rows:
        both[0] = rows[0][pl.ds(pl.multiple_of(place_ref[2] * ROWS, ROWS), ROWS)]
    total[...] += lax.dot_general(
        jnp.concatenate(both, axis=0), weights[...], (((1,), (1,)), ((), ())), preferred_element_type=jnp.float32
    )

    @pl.when(step == pl.num_programs(0) - 1)
    def _():
        base = 0
        for out in outs:
            out[...] = total[base : base + out.shape[0]].astype(jnp.bfloat16)
            base += out.shape[0]


def project(place, weights, arrays, own_rows=False):
    width = weights.shape[0]
    heights = [array.shape[0] for array in arrays]
    if own_rows:
        heights[0] = ROWS
    return pl.pallas_call(
        functools.partial(project_kernel, len(arrays), own_rows),
        out_shape=[jax.ShapeDtypeStruct((height, width), jnp.bfloat16) for height in heights],
        grid_spec=pltpu.PrefetchScalarGridSpec(
            num_scalar_prefetch=1,
            grid=(D // KSTEP,),
            in_specs=[pl.BlockSpec((array.shape[0], KSTEP), lambda step, _: (0, step)) for array in arrays]
            + [pl.BlockSpec((width, KSTEP), lambda step, _: (0, step))],
            out_specs=[pl.BlockSpec((height, width), lambda step, _: (0, 0)) for height in heights],
            scratch_shapes=[pltpu.VMEM((sum(heights), width), jnp.float32)],
        ),
        compiler_params=pltpu.CompilerParams(vmem_limit_bytes=255 * 2**18),
        cost_estimate=pl.CostEstimate(
            flops=2 * sum(heights) * width * D, bytes_accessed=2 * D * (sum(heights) + width), transcendentals=0
        ),
    )(place, *arrays, weights)


def attend_kernel(*refs):
    (order, plen, rlen, spot_z, cosf, sinf, qgain, kgain) = refs[:8]
    pages = refs[8:16]
    resp = refs[16:18]
    near_cols, far_cols = refs[18], refs[19]
    turned_cols = refs[20:26]
    out = refs[26]
    cols, kv, rkv, queries, mixed, sem_c, sem_kv, sem_r = refs[27:]
    core = spot_z[2]
    mine = pl.ds(pl.multiple_of(core * ROWS, ROWS), ROWS)
    place = spot_z[5]
    pltpu.make_async_copy(near_cols, cols.at[place], sem_c).start()
    pltpu.make_async_copy(far_cols, cols.at[(place + 4) % 8], sem_c).start()
    for k in range(3):
        ahead = (k + 1) * (1 - 2 * core)
        pltpu.make_async_copy(turned_cols[2 * k].at[mine], cols.at[(place + ahead + 8) % 8], sem_c).start()
        pltpu.make_async_copy(turned_cols[2 * k + 1].at[mine], cols.at[(place - ahead + 8) % 8], sem_c).start()
    pltpu.make_async_copy(cols, cols, sem_c).wait()
    for n in range(HELD):
        j = n // 4 * 4 + (0, 3 - 2 * core, 1 + 2 * core, 2)[n % 4]
        pltpu.make_async_copy(pages[n], kv.at[j], sem_kv.at[j]).start()
    for j in range(HELD):
        for a, sample in enumerate((core, 1 - core)):
            pltpu.make_async_copy(resp[a].at[order[j]], rkv.at[2 * j + sample, pl.ds(0, RL)], sem_r.at[j]).start()

    low = lax.broadcasted_iota(jnp.int32, (ROWS, HD), 1) < 64

    def head_of(hh):
        half, even, n = hh // 20, hh % 20 // 5 * 2, hh % 5
        if n < 2:
            return cols[even, :, half * 256 + n * HD : half * 256 + (n + 1) * HD].astype(jnp.float32)
        if n > 2:
            return cols[even + 1, :, half * 256 + (n - 3) * HD : half * 256 + (n - 2) * HD].astype(jnp.float32)
        left = cols[even, :, 512:640].astype(jnp.float32)
        right = cols[even + 1, :, 512:640].astype(jnp.float32)
        if half == 0:
            return jnp.where(low, left, pltpu.roll(right, 64, 1))
        return jnp.where(low, pltpu.roll(left, 64, 1), right)

    cosine, sine = cosf[...], sinf[...]

    def turned(hh, gain):
        head = head_of(hh)
        mean = jnp.mean(head * head, axis=-1, keepdims=True)
        head = head * lax.rsqrt(mean + 1e-6) * gain
        return (head * cosine + pltpu.roll(head, 64, 1) * sine).astype(jnp.bfloat16)

    fresh = [turned(HEADS + k, kgain[...]) for k in range(KV_HEADS)]
    fresh += [head_of(HEADS + KV_HEADS + k).astype(jnp.bfloat16) for k in range(KV_HEADS)]
    for k in range(2 * KV_HEADS):
        for n in range(SLOTS):
            rkv[n, RL:RK, k * HD : (k + 1) * HD] = fresh[k][n // 4 * NEW : (n // 4 + 1) * NEW]
    for h in range(HEADS):
        queries[h] = turned(h, qgain[...]).astype(jnp.float32)

    key_p = lax.broadcasted_iota(jnp.int32, (PLEN, 2 * HD), 0)
    key_r = lax.broadcasted_iota(jnp.int32, (RK, 2 * HD), 0)
    lane = lax.broadcasted_iota(jnp.int32, (RK, 2 * HD), 1)
    first = lane // STEPS % 2 == 0
    spot = key_r - RL
    seen = (spot >= 0) & (spot % STEPS <= lane % STEPS)
    turn = spot // STEPS
    first_row = lax.broadcasted_iota(jnp.int32, (2 * STEPS * GROUP, HD), 0) // STEPS % 2 == 0
    across = (((1,), (1,)), ((), ()))
    down = (((0,), (0,)), ((), ()))
    factor = SCALE * 1.4426950408889634
    wide = 2 * STEPS * GROUP
    zero = jnp.zeros((wide, HD), jnp.float32)

    def one_slot(j):
        rows = pl.ds(j * 2 * STEPS, 2 * STEPS)
        spread = []
        for k in range(KV_HEADS):
            q = queries[k * GROUP : (k + 1) * GROUP, rows, :].reshape(wide, HD)
            spread.append(jnp.concatenate([q if n == k else zero for n in range(KV_HEADS)], axis=1))
        q = jnp.concatenate(spread, axis=0).astype(jnp.bfloat16)
        s_p = lax.dot_general(kv[j, :, :KVD], q, across, preferred_element_type=jnp.float32)
        s_p = jnp.where(key_p < plen[j], s_p, -1e30)
        s_r = []
        for a in range(2):
            one = lax.dot_general(rkv[2 * j + a, :, :KVD], q, across, preferred_element_type=jnp.float32)
            s_r.append(jnp.where((key_r < rlen[2 * j + a]) | (seen & (turn == (2 * j + a) % 4)), one, -1e30))
        s_r = jnp.where(first, s_r[0], s_r[1])
        peak = jnp.maximum(jnp.max(s_p, axis=0, keepdims=True), jnp.max(s_r, axis=0, keepdims=True))
        w_p = jnp.exp2((s_p - peak) * factor)
        w_r = jnp.exp2((s_r - peak) * factor)
        share = 1.0 / (jnp.sum(w_p, axis=0, keepdims=True) + jnp.sum(w_r, axis=0, keepdims=True))
        w_p = (w_p * share).astype(jnp.bfloat16)
        w_r = (w_r * share).astype(jnp.bfloat16)
        for pair in range(2):
            lanes = slice(pair * 2 * wide, (pair + 1) * 2 * wide)
            feats = slice(KVD + pair * 2 * HD, KVD + (pair + 1) * 2 * HD)
            mix = lax.dot_general(w_p[:, lanes], kv[j, :, feats], down, preferred_element_type=jnp.float32)
            mix_r = [
                lax.dot_general(w_r[:, lanes], rkv[2 * j + a, :, feats], down, preferred_element_type=jnp.float32)
                for a in range(2)
            ]
            for n in range(2):
                k = 2 * pair + n
                block = (slice(n * wide, (n + 1) * wide), slice(n * HD, (n + 1) * HD))
                one = mix[block] + jnp.where(first_row, mix_r[0][block], mix_r[1][block])
                mixed[k * GROUP : (k + 1) * GROUP, rows, :] = one.reshape(GROUP, 2 * STEPS, HD)

    def some_slots(i, carry):
        for n in range(BATCH):
            j = i * BATCH + n
            pltpu.make_async_copy(kv.at[j], kv.at[j], sem_kv.at[j]).wait()
            both = rkv.at[pl.ds(2 * j, 2), pl.ds(0, RL)]
            pltpu.make_async_copy(both, both, sem_r.at[j]).wait()
        for n in range(BATCH):
            one_slot(i * BATCH + n)
        return carry

    lax.fori_loop(0, HELD // BATCH, some_slots, 0)
    for h in range(HEADS):
        out[:, h * HD : (h + 1) * HD] = mixed[h].astype(jnp.bfloat16)


BATCH = 2


def attend_all(order, plen, rlen, spot_z, cosf, sinf, qgain, kgain, pages, resp, pieces):
    vmem = pl.BlockSpec(memory_space=pltpu.VMEM)
    smem = pl.BlockSpec(memory_space=pltpu.SMEM)
    hbm = pl.BlockSpec(memory_space=pl.ANY)
    return pl.pallas_call(
        attend_kernel,
        out_shape=jax.ShapeDtypeStruct((ROWS, QD), jnp.bfloat16),
        in_specs=[smem] * 4 + [vmem] * 4 + [hbm] * 18,
        out_specs=vmem,
        scratch_shapes=[
            pltpu.VMEM((8, ROWS, 640), jnp.bfloat16),
            pltpu.VMEM((HELD, PLEN, 2 * KVD), jnp.bfloat16),
            pltpu.VMEM((SLOTS, RK, 2 * KVD), jnp.bfloat16),
            pltpu.VMEM((HEADS, ROWS, HD), jnp.float32),
            pltpu.VMEM((HEADS, ROWS, HD), jnp.float32),
            pltpu.SemaphoreType.DMA,
            pltpu.SemaphoreType.DMA((HELD,)),
            pltpu.SemaphoreType.DMA((HELD,)),
        ],
        compiler_params=pltpu.CompilerParams(vmem_limit_bytes=255 * 2**18),
        cost_estimate=pl.CostEstimate(
            flops=4 * ROWS * QD * (PLEN + RK), bytes_accessed=13 * 2**20, transcendentals=ROWS * HEADS * (PLEN + RK)
        ),
    )(order, plen, rlen, spot_z, cosf, sinf, qgain, kgain, *pages, *resp, *pieces)


def shift(array, axis, size, by):
    return lax.ppermute(array, axis, [(i, (i + by) % size) for i in range(size)])


def turn(array, axis, size, by):
    pairs = []
    for n in range(size):
        for c in range(2):
            pairs.append((n * 2 + c, (n + (by if c == 0 else -by)) % size * 2 + c))
    return lax.ppermute(array, (axis, "c"), pairs)


def swap_block(part):
    pairs = []
    for yl in range(2):
        for yh in range(2):
            for c in range(2):
                pairs.append((yl * 4 + yh * 2 + c, (1 - yl) * 4 + (yh ^ c) * 2 + c))
    return lax.ppermute(part, ("yl", "yh", "c"), pairs)


def per_device(
    hidden,
    norm_gain,
    w_qkv,
    query_gain,
    key_gain,
    prompt_kv,
    block_table,
    prompt_slot,
    prompt_len,
    resp_kv,
    resp_len,
):
    yl, z, yh, x, c = (lax.axis_index(name) for name in FSDP + SAMPLE)
    place = jnp.stack([yh, x, c, yl, z % 2, z]).astype(jnp.int32)
    step = lax.optimization_barrier
    mine = hidden.reshape(ROWS, D)
    mate = shift(mine, "c", 2, 1)
    mate_len = shift(resp_len, "c", 2, 1)
    own_w = w_qkv.T
    normed, part, own = prepare(
        place, block_table[0, 0], prompt_slot, norm_gain.reshape(1, D), mine, mate, own_w, prompt_kv[0]
    )
    resp = resp_kv.reshape(SLOTS, RL, 2 * KVD)

    normed, part, own, resp, mate_len = step((normed, part, own, resp, mate_len))
    rows_1 = turn(normed, "z", 8, 1)
    near = swap_block(part)
    page_a = turn(own, "x", 4, 1)
    mate_resp = shift(resp, "c", 2, 1)

    rows_1, near, page_a, mate_resp = step((rows_1, near, page_a, mate_resp))
    rows_2 = turn(rows_1, "z", 8, 1)
    far = shift(near, "c", 2, 1)
    page_far = turn(page_a, "x", 4, 1)
    other_a = shift(own[: PLEN // 2], "yh", 2, 1)
    weights = join_weights(place, own_w, near, far)
    own_cols, back_1 = project(place, weights, [normed, rows_1], True)

    rows_2, page_far, weights, back_1, other_a, slots, own = step(
        (rows_2, page_far, weights, back_1, other_a, prompt_slot, own)
    )
    other_b = shift(own[PLEN // 2 :], "yh", 2, 1)
    rows_3 = turn(rows_2, "z", 8, 1)
    page_b = turn(own, "x", 4, -1)
    page_e = shift(page_far, "yh", 2, 1)
    cols_1 = turn(back_1, "z", 8, -1)
    (back_2,) = project(place, weights, [rows_2])

    want = slot_of(jnp.arange(HELD, dtype=jnp.int32), yh, x, c)
    hit = (slots == want[:, None]).astype(jnp.int32)
    order = jnp.sum(hit * jnp.arange(SLOTS, dtype=jnp.int32)[None, :], axis=1)
    plen = jnp.sum(hit * prompt_len, axis=1)
    lens = jnp.where(c == 0, jnp.concatenate([resp_len, mate_len], axis=1), jnp.concatenate([mate_len, resp_len], axis=1))
    rlen = jnp.sum(hit[:, :, None] * lens[None], axis=1)
    positions = (plen[:, None] + rlen)[:, :, None] + jnp.arange(STEPS, dtype=jnp.int32)
    rlen = rlen.reshape(SLOTS)
    inv_freq = jnp.exp(-jnp.log(1000000.0) * jnp.arange(HD // 2, dtype=jnp.float32) * 2.0 / HD)
    angles = positions.reshape(ROWS, 1).astype(jnp.float32) * inv_freq[None, :]
    cosine, sine = jnp.cos(angles), jnp.sin(angles)
    cosf = jnp.concatenate([cosine, cosine], axis=1)
    sinf = jnp.concatenate([-sine, sine], axis=1)


    rows_3, page_b, other_b, back_2, cols_1, order, plen, rlen, cosf, sinf = step(
        (rows_3, page_b, other_b, back_2, cols_1, order, plen, rlen, cosf, sinf)
    )
    other = jnp.concatenate([other_a, other_b], axis=0)
    rows_4 = turn(lax.dynamic_slice_in_dim(rows_3, c * ROWS, ROWS, 0), "z", 8, 1)
    page_c = turn(other, "x", 4, 1)
    page_d = turn(other, "x", 4, -1)
    cols_2 = turn(back_2, "z", 8, -2)

    back_3, back_4 = project(place, weights, [rows_3, rows_4])
    cols_3 = turn(back_3, "z", 8, -3)
    cols_4 = turn(back_4, "z", 8, -4)
    cols_3, cols_4 = step((cols_3, cols_4))
    turned = []
    for cols in (cols_1, cols_2, cols_3):
        turned += [cols, shift(cols, "c", 2, 1)]

    kept = attend_all(
        order,
        plen,
        rlen,
        place,
        cosf,
        sinf,
        query_gain.reshape(1, HD),
        key_gain.reshape(1, HD),
        [own, page_a, page_b, page_far, other, page_c, page_d, page_e],
        (resp, mate_resp),
        [own_cols, cols_4] + turned,
    )
    got = shift(kept, "c", 2, 1)
    return rows_back(place, prompt_slot, kept, got).reshape(STEPS, SLOTS, 1, QD)


def solution(mesh):
    fine = Mesh(np.asarray(mesh.devices).reshape(2, 8, 2, 4, 2), FSDP + SAMPLE)
    placed = (
        P(None, FSDP, SAMPLE, None),
        P(),
        P(None, FSDP),
        P(),
        P(),
        P(FSDP, SAMPLE, None, None),
        P(FSDP, SAMPLE, None),
        P(FSDP, None),
        P(FSDP, None),
        P(FSDP, SAMPLE, None, None),
        P(FSDP, SAMPLE),
    )
    return jax.shard_map(
        per_device,
        mesh=fine,
        in_specs=placed,
        out_specs=P(None, FSDP, SAMPLE, None),
        check_vma=False,
    )
```

```python
import functools

import jax
import jax.numpy as jnp
import numpy as np
from jax import lax
from jax.experimental import pallas as pl
from jax.experimental.pallas import tpu as pltpu
from jax.sharding import Mesh, PartitionSpec as P

D = 5120
HD = 128
HEADS = 32
KV_HEADS = 4
GROUP = HEADS // KV_HEADS
QD = 4096
KVD = 512
STEPS = 4
SLOTS = 16
HELD = SLOTS // 2
ROWS = STEPS * SLOTS
PLEN = 512
RL = 128
NEW = 16
RK = RL + NEW
SCALE = HD**-0.5
FSDP = ("yl", "z")
SAMPLE = ("yh", "x", "c")


def slot_of(j, yh, x, c):
    return (((j // 4) ^ yh) * 4 + (x + j % 4) % 4) * 2 + c


def prepare_kernel(
    place_ref, table_ref, slots_ref, gain_ref, mine_ref, mate_ref, weights, pool, normed_ref, part_ref, pages_ref, sem
):
    depth = pl.ds(pl.multiple_of(place_ref[2] * (D // 2), 128), D // 2)
    copies = [pltpu.make_async_copy(weights.at[:, depth], part_ref, sem.at[8])]
    for n in range(8):
        copies.append(pltpu.make_async_copy(pool.at[table_ref[n]], pages_ref.at[pl.ds(n * 64, 64)], sem.at[n]))
    for copy in copies:
        copy.start()
    row = lax.broadcasted_iota(jnp.int32, (2 * ROWS, ROWS), 0)
    col = lax.broadcasted_iota(jnp.int32, (2 * ROWS, ROWS), 1)
    want = slot_of(row % ROWS // (2 * STEPS), place_ref[0], place_ref[1], row // ROWS)
    have = jnp.concatenate([slots_ref[...]] * STEPS, axis=1)
    hit = (want == have) & (row % STEPS == col // SLOTS)
    own = row // STEPS % 2 == place_ref[2]
    pick = jnp.concatenate([jnp.where(hit & own, 1.0, 0.0), jnp.where(hit & ~own, 1.0, 0.0)], axis=1)
    both = jnp.concatenate([mine_ref[...], mate_ref[...]], axis=0)
    wide = jnp.dot(pick.astype(jnp.bfloat16), both, preferred_element_type=jnp.float32)
    mean = jnp.mean(wide * wide, axis=-1, keepdims=True)
    normed_ref[...] = (wide * lax.rsqrt(mean + 1e-6) * gain_ref[...]).astype(jnp.bfloat16)
    for copy in copies:
        copy.wait()


def prepare(place, table, slots, gain, mine, mate, weights, pool):
    vmem = pl.BlockSpec(memory_space=pltpu.VMEM)
    smem = pl.BlockSpec(memory_space=pltpu.SMEM)
    hbm = pl.BlockSpec(memory_space=pl.ANY)
    return pl.pallas_call(
        prepare_kernel,
        out_shape=(
            jax.ShapeDtypeStruct((2 * ROWS, D), jnp.bfloat16),
            jax.ShapeDtypeStruct((weights.shape[0], D // 2), jnp.bfloat16),
            jax.ShapeDtypeStruct((PLEN, 2 * KVD), jnp.bfloat16),
        ),
        in_specs=[smem, smem, vmem, vmem, vmem, vmem, hbm, hbm],
        out_specs=(vmem, vmem, vmem),
        scratch_shapes=[pltpu.SemaphoreType.DMA((9,))],
        compiler_params=pltpu.CompilerParams(vmem_limit_bytes=255 * 2**18),
        cost_estimate=pl.CostEstimate(flops=8 * ROWS * ROWS * D, bytes_accessed=8 * 2**20, transcendentals=0),
    )(place, table, slots, gain, mine, mate, weights, pool)


def back_kernel(place_ref, slots_ref, kept_ref, got_ref, out_ref):
    row = lax.broadcasted_iota(jnp.int32, (ROWS, ROWS), 0)
    col = lax.broadcasted_iota(jnp.int32, (ROWS, ROWS), 1)
    have = jnp.concatenate([slots_ref[...]] * STEPS, axis=1)
    turn = (row % STEPS == col // SLOTS) & (row // STEPS % 2 == place_ref[2])
    down = (((0,), (0,)), ((), ()))
    total = jnp.zeros(out_ref.shape, jnp.float32)
    for core, ref in ((place_ref[2], kept_ref), (1 - place_ref[2], got_ref)):
        want = slot_of(row // (2 * STEPS), place_ref[0], place_ref[1], core)
        hit = jnp.where((want == have) & turn, 1.0, 0.0).astype(jnp.bfloat16)
        total += lax.dot_general(hit, ref[...], down, preferred_element_type=jnp.float32)
    out_ref[...] = total.astype(jnp.bfloat16)


def rows_back(place, slots, kept, got):
    vmem = pl.BlockSpec(memory_space=pltpu.VMEM)
    return pl.pallas_call(
        back_kernel,
        out_shape=jax.ShapeDtypeStruct((ROWS, QD), jnp.bfloat16),
        in_specs=[pl.BlockSpec(memory_space=pltpu.SMEM), vmem, vmem, vmem],
        out_specs=vmem,
        compiler_params=pltpu.CompilerParams(vmem_limit_bytes=255 * 2**18),
        cost_estimate=pl.CostEstimate(flops=4 * ROWS * ROWS * QD, bytes_accessed=4 * ROWS * QD, transcendentals=0),
    )(place, slots, kept, got)


KSTEP = 2560


def join_kernel(place_ref, own, near, far, out, sem):
    c, yl, odd = place_ref[2], place_ref[3], place_ref[4]
    head = pl.ds(pl.multiple_of(odd * 64, 64), 256)
    tail = pl.ds(pl.multiple_of((1 - odd) * 256, 64), 64)

    def to(which, size):
        base = which * 256 if size == 256 else 512 + which * 64
        return pl.ds(pl.multiple_of(base, 64), size)

    copies = []
    for rows in (head, tail):
        size = rows.size
        copies.append((own.at[rows], out.at[to(yl, size)]))
        for block, half in ((near, c), (far, 1 - c)):
            depth = pl.ds(pl.multiple_of(half * (D // 2), 128), D // 2)
            copies.append((block.at[rows], out.at[to(1 - yl, size), depth]))
    copies = [pltpu.make_async_copy(src, dst, sem.at[n]) for n, (src, dst) in enumerate(copies)]
    for copy in copies:
        copy.start()
    for copy in copies:
        copy.wait()


def join_weights(place, own_w, near, far):
    hbm = pl.BlockSpec(memory_space=pl.ANY)
    return pl.pallas_call(
        join_kernel,
        out_shape=jax.ShapeDtypeStruct((2 * own_w.shape[0], D), jnp.bfloat16),
        in_specs=[pl.BlockSpec(memory_space=pltpu.SMEM), hbm, hbm, hbm],
        out_specs=pl.BlockSpec(memory_space=pltpu.VMEM),
        scratch_shapes=[pltpu.SemaphoreType.DMA((6,))],
        compiler_params=pltpu.CompilerParams(vmem_limit_bytes=62 * 2**20),
        cost_estimate=pl.CostEstimate(flops=0, bytes_accessed=8 * D * own_w.shape[0], transcendentals=0),
    )(place, own_w, near, far)


def project_kernel(count, own_rows, *refs):
    place_ref, rows, weights, outs, total = refs[0], refs[1 : 1 + count], refs[1 + count], refs[2 + count : -1], refs[-1]
    step = pl.program_id(0)

    @pl.when(step == 0)
    def _():
        total[...] = jnp.zeros_like(total)

    both = [ref[...] for ref in rows]
    if own_rows:
        both[0] = rows[0][pl.ds(pl.multiple_of(place_ref[2] * ROWS, ROWS), ROWS)]
    total[...] += lax.dot_general(
        jnp.concatenate(both, axis=0), weights[...], (((1,), (1,)), ((), ())), preferred_element_type=jnp.float32
    )

    @pl.when(step == pl.num_programs(0) - 1)
    def _():
        base = 0
        for out in outs:
            out[...] = total[base : base + out.shape[0]].astype(jnp.bfloat16)
            base += out.shape[0]


def project(place, weights, arrays, own_rows=False):
    width = weights.shape[0]
    heights = [array.shape[0] for array in arrays]
    if own_rows:
        heights[0] = ROWS
    return pl.pallas_call(
        functools.partial(project_kernel, len(arrays), own_rows),
        out_shape=[jax.ShapeDtypeStruct((height, width), jnp.bfloat16) for height in heights],
        grid_spec=pltpu.PrefetchScalarGridSpec(
            num_scalar_prefetch=1,
            grid=(D // KSTEP,),
            in_specs=[pl.BlockSpec((array.shape[0], KSTEP), lambda step, _: (0, step)) for array in arrays]
            + [pl.BlockSpec((width, KSTEP), lambda step, _: (0, step))],
            out_specs=[pl.BlockSpec((height, width), lambda step, _: (0, 0)) for height in heights],
            scratch_shapes=[pltpu.VMEM((sum(heights), width), jnp.float32)],
        ),
        compiler_params=pltpu.CompilerParams(vmem_limit_bytes=62 * 2**20),
        cost_estimate=pl.CostEstimate(
            flops=2 * sum(heights) * width * D, bytes_accessed=2 * D * (sum(heights) + width), transcendentals=0
        ),
    )(place, *arrays, weights)


def attend_kernel(*refs):
    (order, plen, rlen, spot_z, cosf, sinf, qgain, kgain) = refs[:8]
    pages = refs[8:16]
    resp = refs[16:18]
    near_cols, far_cols = refs[18], refs[19]
    turned_cols = refs[20:26]
    out = refs[26]
    cols, kv, rkv, queries, mixed, sem_c, sem_kv, sem_r = refs[27:]
    core = spot_z[2]
    mine = pl.ds(pl.multiple_of(core * ROWS, ROWS), ROWS)
    place = spot_z[5]
    pltpu.make_async_copy(near_cols, cols.at[place], sem_c).start()
    pltpu.make_async_copy(far_cols, cols.at[(place + 4) % 8], sem_c).start()
    for k in range(3):
        ahead = (k + 1) * (1 - 2 * core)
        pltpu.make_async_copy(turned_cols[2 * k].at[mine], cols.at[(place + ahead + 8) % 8], sem_c).start()
        pltpu.make_async_copy(turned_cols[2 * k + 1].at[mine], cols.at[(place - ahead + 8) % 8], sem_c).start()
    pltpu.make_async_copy(cols, cols, sem_c).wait()
    for n in range(HELD):
        j = n // 4 * 4 + (0, 3 - 2 * core, 1 + 2 * core, 2)[n % 4]
        pltpu.make_async_copy(pages[n], kv.at[j], sem_kv.at[j]).start()
    for j in range(HELD):
        for a, sample in enumerate((core, 1 - core)):
            pltpu.make_async_copy(resp[a].at[order[j]], rkv.at[2 * j + sample, pl.ds(0, RL)], sem_r.at[j]).start()

    low = lax.broadcasted_iota(jnp.int32, (ROWS, HD), 1) < 64

    def head_of(hh):
        half, even, n = hh // 20, hh % 20 // 5 * 2, hh % 5
        if n < 2:
            return cols[even, :, half * 256 + n * HD : half * 256 + (n + 1) * HD].astype(jnp.float32)
        if n > 2:
            return cols[even + 1, :, half * 256 + (n - 3) * HD : half * 256 + (n - 2) * HD].astype(jnp.float32)
        left = cols[even, :, 512:640].astype(jnp.float32)
        right = cols[even + 1, :, 512:640].astype(jnp.float32)
        if half == 0:
            return jnp.where(low, left, pltpu.roll(right, 64, 1))
        return jnp.where(low, pltpu.roll(left, 64, 1), right)

    cosine, sine = cosf[...], sinf[...]

    def turned(hh, gain):
        head = head_of(hh)
        mean = jnp.mean(head * head, axis=-1, keepdims=True)
        head = head * lax.rsqrt(mean + 1e-6) * gain
        return (head * cosine + pltpu.roll(head, 64, 1) * sine).astype(jnp.bfloat16)

    fresh = [turned(HEADS + k, kgain[...]) for k in range(KV_HEADS)]
    fresh += [head_of(HEADS + KV_HEADS + k).astype(jnp.bfloat16) for k in range(KV_HEADS)]
    for k in range(2 * KV_HEADS):
        for n in range(SLOTS):
            rkv[n, RL:RK, k * HD : (k + 1) * HD] = fresh[k][n // 4 * NEW : (n // 4 + 1) * NEW]
    for h in range(HEADS):
        queries[h] = turned(h, qgain[...]).astype(jnp.float32)

    key_p = lax.broadcasted_iota(jnp.int32, (PLEN, 2 * HD), 0)
    key_r = lax.broadcasted_iota(jnp.int32, (RK, 2 * HD), 0)
    lane = lax.broadcasted_iota(jnp.int32, (RK, 2 * HD), 1)
    first = lane // STEPS % 2 == 0
    spot = key_r - RL
    seen = (spot >= 0) & (spot % STEPS <= lane % STEPS)
    turn = spot // STEPS
    first_row = lax.broadcasted_iota(jnp.int32, (2 * STEPS * GROUP, HD), 0) // STEPS % 2 == 0
    across = (((1,), (1,)), ((), ()))
    down = (((0,), (0,)), ((), ()))
    factor = SCALE * 1.4426950408889634
    wide = 2 * STEPS * GROUP
    zero = jnp.zeros((wide, HD), jnp.float32)

    def one_slot(j):
        rows = pl.ds(j * 2 * STEPS, 2 * STEPS)
        spread = []
        for k in range(KV_HEADS):
            q = queries[k * GROUP : (k + 1) * GROUP, rows, :].reshape(wide, HD)
            spread.append(jnp.concatenate([q if n == k else zero for n in range(KV_HEADS)], axis=1))
        q = jnp.concatenate(spread, axis=0).astype(jnp.bfloat16)
        s_p = lax.dot_general(kv[j, :, :KVD], q, across, preferred_element_type=jnp.float32)
        s_p = jnp.where(key_p < plen[j], s_p, -1e30)
        s_r = []
        for a in range(2):
            one = lax.dot_general(rkv[2 * j + a, :, :KVD], q, across, preferred_element_type=jnp.float32)
            s_r.append(jnp.where((key_r < rlen[2 * j + a]) | (seen & (turn == (2 * j + a) % 4)), one, -1e30))
        s_r = jnp.where(first, s_r[0], s_r[1])
        peak = jnp.maximum(jnp.max(s_p, axis=0, keepdims=True), jnp.max(s_r, axis=0, keepdims=True))
        w_p = jnp.exp2((s_p - peak) * factor)
        w_r = jnp.exp2((s_r - peak) * factor)
        share = 1.0 / (jnp.sum(w_p, axis=0, keepdims=True) + jnp.sum(w_r, axis=0, keepdims=True))
        w_p = (w_p * share).astype(jnp.bfloat16)
        w_r = (w_r * share).astype(jnp.bfloat16)
        for pair in range(2):
            lanes = slice(pair * 2 * wide, (pair + 1) * 2 * wide)
            feats = slice(KVD + pair * 2 * HD, KVD + (pair + 1) * 2 * HD)
            mix = lax.dot_general(w_p[:, lanes], kv[j, :, feats], down, preferred_element_type=jnp.float32)
            mix_r = [
                lax.dot_general(w_r[:, lanes], rkv[2 * j + a, :, feats], down, preferred_element_type=jnp.float32)
                for a in range(2)
            ]
            for n in range(2):
                k = 2 * pair + n
                block = (slice(n * wide, (n + 1) * wide), slice(n * HD, (n + 1) * HD))
                one = mix[block] + jnp.where(first_row, mix_r[0][block], mix_r[1][block])
                mixed[k * GROUP : (k + 1) * GROUP, rows, :] = one.reshape(GROUP, 2 * STEPS, HD)

    def some_slots(i, carry):
        for n in range(BATCH):
            j = i * BATCH + n
            pltpu.make_async_copy(kv.at[j], kv.at[j], sem_kv.at[j]).wait()
            both = rkv.at[pl.ds(2 * j, 2), pl.ds(0, RL)]
            pltpu.make_async_copy(both, both, sem_r.at[j]).wait()
        for n in range(BATCH):
            one_slot(i * BATCH + n)
        return carry

    lax.fori_loop(0, HELD // BATCH, some_slots, 0)
    for h in range(HEADS):
        out[:, h * HD : (h + 1) * HD] = mixed[h].astype(jnp.bfloat16)


BATCH = 2


def attend_all(order, plen, rlen, spot_z, cosf, sinf, qgain, kgain, pages, resp, pieces):
    vmem = pl.BlockSpec(memory_space=pltpu.VMEM)
    smem = pl.BlockSpec(memory_space=pltpu.SMEM)
    hbm = pl.BlockSpec(memory_space=pl.ANY)
    return pl.pallas_call(
        attend_kernel,
        out_shape=jax.ShapeDtypeStruct((ROWS, QD), jnp.bfloat16),
        in_specs=[smem] * 4 + [vmem] * 4 + [hbm] * 18,
        out_specs=vmem,
        scratch_shapes=[
            pltpu.VMEM((8, ROWS, 640), jnp.bfloat16),
            pltpu.VMEM((HELD, PLEN, 2 * KVD), jnp.bfloat16),
            pltpu.VMEM((SLOTS, RK, 2 * KVD), jnp.bfloat16),
            pltpu.VMEM((HEADS, ROWS, HD), jnp.float32),
            pltpu.VMEM((HEADS, ROWS, HD), jnp.float32),
            pltpu.SemaphoreType.DMA,
            pltpu.SemaphoreType.DMA((HELD,)),
            pltpu.SemaphoreType.DMA((HELD,)),
        ],
        compiler_params=pltpu.CompilerParams(vmem_limit_bytes=62 * 2**20),
        cost_estimate=pl.CostEstimate(
            flops=4 * ROWS * QD * (PLEN + RK), bytes_accessed=13 * 2**20, transcendentals=ROWS * HEADS * (PLEN + RK)
        ),
    )(order, plen, rlen, spot_z, cosf, sinf, qgain, kgain, *pages, *resp, *pieces)


def shift(array, axis, size, by):
    return lax.ppermute(array, axis, [(i, (i + by) % size) for i in range(size)])


def turn(array, axis, size, by):
    pairs = []
    for n in range(size):
        for c in range(2):
            pairs.append((n * 2 + c, (n + (by if c == 0 else -by)) % size * 2 + c))
    return lax.ppermute(array, (axis, "c"), pairs)


def swap_block(part):
    pairs = []
    for yl in range(2):
        for yh in range(2):
            for c in range(2):
                pairs.append((yl * 4 + yh * 2 + c, (1 - yl) * 4 + (yh ^ c) * 2 + c))
    return lax.ppermute(part, ("yl", "yh", "c"), pairs)


def per_device(
    hidden,
    norm_gain,
    w_qkv,
    query_gain,
    key_gain,
    prompt_kv,
    block_table,
    prompt_slot,
    prompt_len,
    resp_kv,
    resp_len,
):
    yl, z, yh, x, c = (lax.axis_index(name) for name in FSDP + SAMPLE)
    place = jnp.stack([yh, x, c, yl, z % 2, z]).astype(jnp.int32)
    step = lax.optimization_barrier
    mine = hidden.reshape(ROWS, D)
    mate = shift(mine, "c", 2, 1)
    mate_len = shift(resp_len, "c", 2, 1)
    own_w = w_qkv.T
    normed, part, own = prepare(
        place, block_table[0, 0], prompt_slot, norm_gain.reshape(1, D), mine, mate, own_w, prompt_kv[0]
    )
    resp = resp_kv.reshape(SLOTS, RL, 2 * KVD)

    normed, part, own, resp, mate_len = step((normed, part, own, resp, mate_len))
    rows_1 = turn(normed, "z", 8, 1)
    near = swap_block(part)
    page_a = turn(own, "x", 4, 1)
    mate_resp = shift(resp, "c", 2, 1)

    rows_1, near, page_a, mate_resp = step((rows_1, near, page_a, mate_resp))
    rows_2 = turn(rows_1, "z", 8, 1)
    far = shift(near, "c", 2, 1)
    page_far = turn(page_a, "x", 4, 1)
    other_a = shift(own[: PLEN // 2], "yh", 2, 1)
    weights = join_weights(place, own_w, near, far)
    own_cols, back_1 = project(place, weights, [normed, rows_1], True)

    rows_2, page_far, weights, back_1, other_a, slots, own = step(
        (rows_2, page_far, weights, back_1, other_a, prompt_slot, own)
    )
    other_b = shift(own[PLEN // 2 :], "yh", 2, 1)
    rows_3 = turn(rows_2, "z", 8, 1)
    page_b = turn(own, "x", 4, -1)
    page_e = shift(page_far, "yh", 2, 1)
    cols_1 = turn(back_1, "z", 8, -1)
    (back_2,) = project(place, weights, [rows_2])

    want = slot_of(jnp.arange(HELD, dtype=jnp.int32), yh, x, c)
    hit = (slots == want[:, None]).astype(jnp.int32)
    order = jnp.sum(hit * jnp.arange(SLOTS, dtype=jnp.int32)[None, :], axis=1)
    plen = jnp.sum(hit * prompt_len, axis=1)
    lens = jnp.where(c == 0, jnp.concatenate([resp_len, mate_len], axis=1), jnp.concatenate([mate_len, resp_len], axis=1))
    rlen = jnp.sum(hit[:, :, None] * lens[None], axis=1)
    positions = (plen[:, None] + rlen)[:, :, None] + jnp.arange(STEPS, dtype=jnp.int32)
    rlen = rlen.reshape(SLOTS)
    inv_freq = jnp.exp(-jnp.log(1000000.0) * jnp.arange(HD // 2, dtype=jnp.float32) * 2.0 / HD)
    angles = positions.reshape(ROWS, 1).astype(jnp.float32) * inv_freq[None, :]
    cosine, sine = jnp.cos(angles), jnp.sin(angles)
    cosf = jnp.concatenate([cosine, cosine], axis=1)
    sinf = jnp.concatenate([-sine, sine], axis=1)


    rows_3, page_b, other_b, back_2, cols_1, order, plen, rlen, cosf, sinf = step(
        (rows_3, page_b, other_b, back_2, cols_1, order, plen, rlen, cosf, sinf)
    )
    other = jnp.concatenate([other_a, other_b], axis=0)
    rows_4 = turn(lax.dynamic_slice_in_dim(rows_3, c * ROWS, ROWS, 0), "z", 8, 1)
    page_c = turn(other, "x", 4, 1)
    page_d = turn(other, "x", 4, -1)
    cols_2 = turn(back_2, "z", 8, -2)

    back_3, back_4 = project(place, weights, [rows_3, rows_4])
    cols_3 = turn(back_3, "z", 8, -3)
    cols_4 = turn(back_4, "z", 8, -4)
    cols_3, cols_4 = step((cols_3, cols_4))
    turned = []
    for cols in (cols_1, cols_2, cols_3):
        turned += [cols, shift(cols, "c", 2, 1)]

    kept = attend_all(
        order,
        plen,
        rlen,
        place,
        cosf,
        sinf,
        query_gain.reshape(1, HD),
        key_gain.reshape(1, HD),
        [own, page_a, page_b, page_far, other, page_c, page_d, page_e],
        (resp, mate_resp),
        [own_cols, cols_4] + turned,
    )
    got = shift(kept, "c", 2, 1)
    return rows_back(place, prompt_slot, kept, got).reshape(STEPS, SLOTS, 1, QD)


def solution(mesh):
    fine = Mesh(np.asarray(mesh.devices).reshape(2, 8, 2, 4, 2), FSDP + SAMPLE)
    placed = (
        P(None, FSDP, SAMPLE, None),
        P(),
        P(None, FSDP),
        P(),
        P(),
        P(FSDP, SAMPLE, None, None),
        P(FSDP, SAMPLE, None),
        P(FSDP, None),
        P(FSDP, None),
        P(FSDP, SAMPLE, None, None),
        P(FSDP, SAMPLE),
    )
    return jax.shard_map(
        per_device,
        mesh=fine,
        in_specs=placed,
        out_specs=P(None, FSDP, SAMPLE, None),
        check_vma=False,
    )
```
